128 devices in a mesh: row: 16 (over z, y), col: 8 (over x, core).
Axes of the slice: x: 4, y: 4, z: 4, core: 2. Of those that a mesh axis runs over, the one named last changes fastest.
Arguments:
- factor: float32 [2, 2048, 2048], P(None, 'row', 'col'), may hold values from -0.09375 to 0.09375
- lower_inverse: float32 [2, 512, 2048], P(None, None, 'row'), may hold values from -1 to 2
- upper_inverse: float32 [2, 512, 2048], P(None, None, 'row'), may hold values from -1 to 2
- krylov_block: float32 [2, 16, 2048], P(None, None, 'row'), may hold values from -6 to 6
- basis: float32 [2, 64, 2048], P(None, None, 'row'), may hold values from -0.09375 to 0.09375
Outputs:
- projected: float32 [2, 16, 2048], P(None, None, 'row')
- coefficients: float32 [2, 64, 16], replicated
The draws below stay inside these ranges and needn't reach their ends.
All inputs are finite; a program needn't handle non-finite values.
Results may differ from the reference program's by a relative error of at most 0.00012.
Values sent between devices are 32-bit elements; how exact they have to be, the bound alone decides.
No kernel may reach another device: no remote copies, remote signals or barrier semaphores. Data moves between devices by JAX's collectives and lax.ppermute only.
A program may use at most 64 MiB of HBM per device.

```python
import jax
import jax.numpy as jnp
from jax import lax

TILE = 512
NRHS = 16
NB = 64
KT = 4
N = 2048


def tile_inverse(key):
    cols = jnp.arange(N) % TILE
    ident = (jnp.arange(TILE)[:, None] == cols[None, :]).astype(jnp.float32)
    noise = jax.random.normal(key, (2, TILE, N), jnp.float32) * (0.3 / jnp.sqrt(jnp.float32(TILE)))
    noise = jnp.clip(noise, -0.2, 0.2)
    return jnp.stack([ident + noise[0], noise[1]])


def draw_lower_inverse(key, part):
    return tile_inverse(jax.random.fold_in(key, 101))


def draw_upper_inverse(key, part):
    return tile_inverse(jax.random.fold_in(key, 202))


def steps_of(rng, shape, split, least, top_value):
    def one(dim, shards_of):
        heights = jax.random.uniform(jax.random.fold_in(jax.random.fold_in(rng, 6), dim), (shards_of,), jnp.float32, least / len(split), top_value / len(split))
        return jnp.repeat(jnp.exp(heights), shape[dim] // shards_of).reshape((-1,) + (1,) * (len(shape) - dim - 1))

    factor_of = one(*split[0])
    for cut in split[1:]:
        factor_of = factor_of * one(*cut)
    return factor_of


def gaussian(stream_key, dims, scale, bound, cuts=(), kind=jnp.bfloat16):
    loudness = steps_of(stream_key, dims, cuts, -0.22, 0.18) if cuts else 1.0
    values = jax.random.normal(stream_key, dims, jnp.float32) * scale * loudness
    return jnp.minimum(jnp.maximum(values, -bound), bound).astype(kind)


def setup_inputs(seed: int = 0) -> dict:
    key_of = jax.random.split(jax.random.key(seed), 6)
    factor = gaussian(key_of[0], (2, N, N), (2 * N) ** -0.5, 0.09375, ((1, 16), (2, 8)), jnp.float32)
    lower_inverse = draw_lower_inverse(jax.random.fold_in(key_of[5], 71), 0)
    upper_inverse = draw_upper_inverse(jax.random.fold_in(key_of[5], 71), 0)
    krylov_block = gaussian(key_of[3], (2, NRHS, N), 1.0, 6.0, ((2, 16),), jnp.float32)
    basis = gaussian(key_of[4], (2, NB, N), (2 * N) ** -0.5, 0.09375, ((2, 16),), jnp.float32)
    return {"factor": factor, "lower_inverse": lower_inverse, "upper_inverse": upper_inverse, "krylov_block": krylov_block, "basis": basis}


def real_dot(left, right):
    return jnp.dot(left, right, preferred_element_type=jnp.float32, precision=lax.Precision.HIGHEST)


def apply_tile(matrix, vectors):
    real_part = real_dot(vectors[0], matrix[0].T) - real_dot(vectors[1], matrix[1].T)
    imag_part = real_dot(vectors[0], matrix[1].T) + real_dot(vectors[1], matrix[0].T)
    return jnp.stack([real_part, imag_part])


def herm_dot(basis_part, vectors):
    real_part = real_dot(basis_part[0], vectors[0].T) + real_dot(basis_part[1], vectors[1].T)
    imag_part = real_dot(basis_part[0], vectors[1].T) - real_dot(basis_part[1], vectors[0].T)
    return jnp.stack([real_part, imag_part])


def combine(basis_part, coeffs):
    real_part = real_dot(coeffs[0].T, basis_part[0]) - real_dot(coeffs[1].T, basis_part[1])
    imag_part = real_dot(coeffs[0].T, basis_part[1]) + real_dot(coeffs[1].T, basis_part[0])
    return jnp.stack([real_part, imag_part])


def sweep(factor, inverse, source, backward):
    start = jnp.zeros(source.shape, jnp.float32)

    def step(index, current):
        k = (KT - 1 - index) if backward else index
        k = jnp.asarray(k).astype(jnp.int32)
        rows = lax.dynamic_slice_in_dim(factor, k * TILE, TILE, 1)
        partial_value = apply_tile(rows, current)
        given = lax.dynamic_slice_in_dim(source, k * TILE, TILE, 2)
        inv = lax.dynamic_slice_in_dim(inverse, k * TILE, TILE, 2)
        piece = apply_tile(inv, given - partial_value)
        return lax.dynamic_update_slice_in_dim(current, piece, k * TILE, 2)

    return lax.fori_loop(0, KT, step, start)


def reference(factor, lower_inverse, upper_inverse, krylov_block, basis):
    solved = sweep(factor, lower_inverse, krylov_block, False)
    solution = sweep(factor, upper_inverse, solved, True)
    first = herm_dot(basis, solution)
    middle = solution - combine(basis, first)
    second = herm_dot(basis, middle)
    projected = middle - combine(basis, second)
    return projected, first + second
```

```python
import jax
import jax.numpy as jnp
from jax import lax
from jax.sharding import Mesh, PartitionSpec as P

SIDE = 4
AXES = ("z", "y", "x", "c")
HIGH = lax.Precision.HIGH
HIGHEST = lax.Precision.HIGHEST


def dot_nt(left, right, precision):
    return lax.dot_general(left, right, (((1,), (1,)), ((), ())), precision=precision, preferred_element_type=jnp.float32)


def apply_rows(vectors, matrix, precision=HIGH):
    n = vectors.shape[1]
    both = jnp.concatenate([vectors[0], vectors[1]], 0)
    by_real = dot_nt(both, matrix[0], precision)
    by_imag = dot_nt(both, matrix[1], precision)
    return jnp.stack([by_real[:n] - by_imag[n:], by_real[n:] + by_imag[:n]])


def herm_rows(vectors, matrix, precision=HIGHEST):
    n = vectors.shape[1]
    both = jnp.concatenate([vectors[0], vectors[1]], 0)
    by_real = dot_nt(both, matrix[0], precision)
    by_imag = dot_nt(both, matrix[1], precision)
    return jnp.stack([by_real[:n] + by_imag[n:], by_real[n:] - by_imag[:n]])


def combine_rows(coeffs, matrix, precision=HIGHEST):
    n = coeffs.shape[1]
    both = jnp.concatenate([coeffs[0], coeffs[1]], 0)
    by_real = jnp.dot(both, matrix[0], precision=precision, preferred_element_type=jnp.float32)
    by_imag = jnp.dot(both, matrix[1], precision=precision, preferred_element_type=jnp.float32)
    return jnp.stack([by_real[:n] - by_imag[n:], by_real[n:] + by_imag[:n]])


def index_of(z, y, x, c):
    return ((z * SIDE + y) * SIDE + x) * 2 + c


def move(value, target):
    pairs = []
    for z in range(SIDE):
        for y in range(SIDE):
            for x in range(SIDE):
                for c in range(2):
                    there = target(z, y, x, c)
                    if there is not None:
                        pairs.append((index_of(z, y, x, c), index_of(*there)))
    return lax.ppermute(value, AXES, pairs)


def swap(value):
    return lax.ppermute(value, "c", [(0, 1), (1, 0)])


def along_y(value, planes, offset):
    def target(z, y, x, c):
        return (z, (y - offset) % SIDE, x, c) if z in planes else None

    return move(value, target)


def along_z(value, source, dest):
    def target(z, y, x, c):
        return (dest, y, x, c) if z == source else None

    return move(value, target)


def spread_x(value, role, offset):
    def target(z, y, x, c):
        return (z, y, (x + offset) % SIDE, c) if x == (z - role) % SIDE else None

    return move(value, target)


def local(factor, lower_inverse, upper_inverse, krylov_block, basis):
    z = lax.axis_index("z")
    y = lax.axis_index("y")
    x = lax.axis_index("x")
    c = lax.axis_index("c")
    piece = factor.shape[1]
    half = factor.shape[2]
    tile = 2 * half
    nvec = krylov_block.shape[1]
    mine = nvec // 2
    every = range(SIDE)

    def role_tile(role):
        own = jnp.where(x == (z - role) % SIDE, factor, 0.0)
        for offset in (1, 3, 2):
            own = own + spread_x(factor, role, offset)
        return own

    roles = {s: role_tile(s) for s in (1, 2, 3)}
    others = {s: swap(roles[s]) for s in (1, 2, 3)}

    def forward_product(vectors, s):
        near = lax.dynamic_slice_in_dim(vectors, c * half, half, 2)
        far = lax.dynamic_slice_in_dim(vectors, (1 - c) * half, half, 2)
        return apply_rows(near, roles[s]) + apply_rows(far, others[s])

    def both_cores(value):
        other = swap(value)
        first = jnp.where(c == 0, value, other)
        second = jnp.where(c == 0, other, value)
        return first, second

    def rotated(value):
        return lax.dynamic_slice_in_dim(jnp.concatenate([value, value], 2), y * piece, tile, 2)

    given = lax.dynamic_slice_in_dim(krylov_block, c * mine, mine, 1)
    rest = given
    solved = jnp.zeros((2, mine, tile), jnp.float32)
    for k in every:
        partial_value = apply_rows(rest, lower_inverse)
        full = partial_value
        for offset in (1, 3, 2):
            full = full + along_y(partial_value, (k,), offset)
        solved = jnp.where(z == k, full, solved)
        for dest in range(k + 1, SIDE):
            rest = rest - forward_product(along_z(full, k, dest), dest - k)

    upper_half = lax.dynamic_slice_in_dim(upper_inverse, c * half, half, 1)
    upper_rows = jnp.concatenate([upper_half] + [along_y(upper_half, every, d) for d in (1, 2, 3)], 2)
    planes_of = {3: (0, 1, 2), 2: (0, 1), 1: (0,)}
    tall = {}
    for s in (3, 2, 1):
        tall[s] = jnp.concatenate([roles[s]] + [along_y(roles[s], planes_of[s], d) for d in (1, 2, 3)], 1)

    basis_all = jnp.stack([basis] + [along_y(basis, every, d) for d in (1, 2, 3)])
    low = lax.dynamic_index_in_dim(basis_all, (2 * c - y) % SIDE, 0, False)
    high = lax.dynamic_index_in_dim(basis_all, (2 * c + 1 - y) % SIDE, 0, False)
    basis_half = jnp.concatenate([low, high], 2)
    gram = herm_rows(basis_half, basis_half)
    gram = gram + swap(gram)
    shifts = [[(i, (i + d) % SIDE) for i in every] for d in (1, 3, 2)]
    gram_parts = [lax.ppermute(gram, "z", s) for s in shifts]
    gram = gram + gram_parts[0] + gram_parts[1] + gram_parts[2]
    nb = basis.shape[1]
    twice = jnp.stack([2.0 * jnp.eye(nb, dtype=jnp.float32), jnp.zeros((nb, nb), jnp.float32)])
    keep = twice - gram
    spread = combine_rows(keep, basis)

    start, end = both_cores(solved)
    held = rotated(jnp.concatenate([start, end], 1))
    acc = jnp.zeros((2, nvec, tile), jnp.float32)
    final = jnp.zeros((2, nvec, half), jnp.float32)
    early = None
    for k in (3, 2, 1, 0):
        if k == 3:
            right = held
        else:
            right = held - (acc + swap(acc))
        part = apply_rows(right, upper_rows)
        if k > 0:
            final = jnp.where(z == k, part, final)
            for dest in range(k - 1, -1, -1):
                acc = acc + apply_rows(along_z(part, k, dest), tall[(dest - k) % SIDE])
        if k == 1:
            early = herm_rows(final, basis_half)
            early = early + swap(early)
            parts = [lax.ppermute(early, "z", s) for s in shifts]
            early = early + parts[0] + parts[1] + parts[2]
            before, after = both_cores(final)
            own_early = jnp.where(y % 2 == 0, 0, piece)
            chosen = jnp.where(y < 2, before, after)
            own_rows = lax.dynamic_slice_in_dim(chosen, own_early, piece, 2)
    last = herm_rows(part, basis_half)
    packed = jnp.concatenate([part, last], 2)
    other = swap(packed)
    last = last + other[:, :, half:]
    from_half = jnp.where((y < 2) == (c == 0), part, other[:, :, :half])
    own_last = lax.dynamic_slice_in_dim(from_half, (y % 2) * piece, piece, 2)
    own_rows = jnp.where(z == 0, own_last, own_rows)
    total = jnp.where(z == 0, last, 0.0)
    for dest in (1, 3, 2):
        total = total + along_z(last, 0, dest)
    first = total + early
    projected = own_rows - combine_rows(first, spread)
    coeffs = combine_rows(first, keep)
    return projected, jnp.swapaxes(coeffs, 1, 2)


def solution(mesh):
    split = Mesh(mesh.devices.reshape(SIDE, SIDE, SIDE, 2), AXES)
    row, col = ("z", "y"), ("x", "c")
    in_specs = (P(None, row, col), P(None, None, row), P(None, None, row), P(None, None, row), P(None, None, row))
    out_specs = (P(None, None, row), P())
    return jax.shard_map(local, mesh=split, in_specs=in_specs, out_specs=out_specs, check_vma=False)
```

```python
import jax
import jax.numpy as jnp
from jax import lax
from jax.sharding import Mesh, PartitionSpec as P

SIDE = 4
AXES = ("z", "y", "x", "c")
HIGH = lax.Precision.HIGH
HIGHEST = lax.Precision.HIGHEST


def dot_nt(left, right, precision):
    return lax.dot_general(left, right, (((1,), (1,)), ((), ())), precision=precision, preferred_element_type=jnp.float32)


def apply_rows(vectors, matrix, precision=HIGH):
    n = vectors.shape[1]
    both = jnp.concatenate([vectors[0], vectors[1]], 0)
    by_real = dot_nt(both, matrix[0], precision)
    by_imag = dot_nt(both, matrix[1], precision)
    return jnp.stack([by_real[:n] - by_imag[n:], by_real[n:] + by_imag[:n]])


def herm_rows(vectors, matrix, precision=HIGHEST):
    n = vectors.shape[1]
    both = jnp.concatenate([vectors[0], vectors[1]], 0)
    by_real = dot_nt(both, matrix[0], precision)
    by_imag = dot_nt(both, matrix[1], precision)
    return jnp.stack([by_real[:n] + by_imag[n:], by_real[n:] - by_imag[:n]])


def combine_rows(coeffs, matrix, precision=HIGHEST):
    n = coeffs.shape[1]
    both = jnp.concatenate([coeffs[0], coeffs[1]], 0)
    by_real = jnp.dot(both, matrix[0], precision=precision, preferred_element_type=jnp.float32)
    by_imag = jnp.dot(both, matrix[1], precision=precision, preferred_element_type=jnp.float32)
    return jnp.stack([by_real[:n] - by_imag[n:], by_real[n:] + by_imag[:n]])


def index_of(z, y, x, c):
    return ((z * SIDE + y) * SIDE + x) * 2 + c


def move(value, target):
    pairs = []
    for z in range(SIDE):
        for y in range(SIDE):
            for x in range(SIDE):
                for c in range(2):
                    there = target(z, y, x, c)
                    if there is not None:
                        pairs.append((index_of(z, y, x, c), index_of(*there)))
    return lax.ppermute(value, AXES, pairs)


def swap(value):
    return lax.ppermute(value, "c", [(0, 1), (1, 0)])


def turn_y(value, offset):
    return move(value, lambda z, y, x, c: (z, (y - offset) % SIDE, x, c))


def hop(value, routes):
    def target(z, y, x, c):
        there = routes.get((z, x))
        return None if there is None else (there[0], y, there[1], c)

    return move(value, target)


def swap_at(value, places):
    return move(value, lambda z, y, x, c: (z, y, x, 1 - c) if (z, x) in places else None)


def local(factor, lower_inverse, upper_inverse, krylov_block, basis):
    z = lax.axis_index("z")
    y = lax.axis_index("y")
    x = lax.axis_index("x")
    c = lax.axis_index("c")
    piece = factor.shape[1]
    half = factor.shape[2]
    tile = 2 * half
    nvec = krylov_block.shape[1]
    nb = basis.shape[1]
    every = range(SIDE)

    def here(*places):
        found = jnp.zeros((), bool)
        for a, b in places:
            found = found | ((z == a) & (x == b))
        return found

    def rotated(value):
        return lax.dynamic_slice_in_dim(jnp.concatenate([value, value], 2), y * piece, tile, 2)

    def in_order(value, other):
        return jnp.concatenate([jnp.where(c == 0, value, other), jnp.where(c == 0, other, value)], 2)

    lower_half = lax.dynamic_slice_in_dim(lower_inverse, c * half, half, 1)
    upper_half = lax.dynamic_slice_in_dim(upper_inverse, c * half, half, 1)

    lead = apply_rows(krylov_block, lower_half)
    gram = herm_rows(basis, basis)
    lead = jnp.concatenate([lead, gram.reshape(2, nvec, half)], 2)
    lead_parts = [turn_y(lead, d) for d in (1, 3, 2)]

    inverse = jnp.where(x == (z + 3) % SIDE, lower_half, upper_half)
    packed = jnp.concatenate([inverse, krylov_block, basis], 1)
    tall = jnp.concatenate([factor] + [turn_y(factor, d) for d in (1, 2, 3)], 1)
    pieces = [packed] + [turn_y(packed, d) for d in (1, 2, 3)]
    rows = jnp.concatenate([p[:, :half] for p in pieces], 2)
    given = jnp.concatenate([p[:, half:half + nvec] for p in pieces], 2)
    basis_all = jnp.stack([p[:, half + nvec:] for p in pieces])
    low = lax.dynamic_index_in_dim(basis_all, (2 * c - y) % SIDE, 0, False)
    high = lax.dynamic_index_in_dim(basis_all, (2 * c + 1 - y) % SIDE, 0, False)
    basis_half = jnp.concatenate([low, high], 2)

    lead = lead + lead_parts[0] + lead_parts[1] + lead_parts[2]
    y0 = lead[:, :, :half]
    gram = lead[:, :, half:].reshape(2, nb, nb)
    shifts = [[(i, (i + d) % SIDE) for i in every] for d in (1, 3, 2)]
    gram_parts = [lax.ppermute(gram, "z", s) for s in shifts]
    gram = gram + gram_parts[0] + gram_parts[1] + gram_parts[2]
    twice = jnp.stack([2.0 * jnp.eye(nb, dtype=jnp.float32), jnp.zeros((nb, nb), jnp.float32)])
    keep = twice - gram
    spread = combine_rows(keep, basis)

    empty = jnp.zeros((2, nvec, half), jnp.float32)
    blank = jnp.zeros((2, nvec, tile), jnp.float32)

    def product(places, vectors, start=None):
        def run(vectors, start, weights):
            out = apply_rows(vectors, weights)
            return out if start is None else start + out

        return lax.cond(here(*places), run, lambda v, s, w: blank, vectors, blank if start is None else start, tall)

    def finish(place, right, acc):
        other = swap_at(acc, (place,))

        def run(right, acc, other, weights):
            return apply_rows(right - (acc + other), weights)

        return lax.cond(here(place), run, lambda r, a, o, w: empty, right, acc, other, rows)

    acc0 = product(((1, 0), (2, 0), (3, 0)), hop(y0, {(0, 0): (1, 0), (0, 1): (2, 0), (0, 3): (3, 0)}))
    y1 = finish((1, 0), given, acc0)
    held0 = hop(acc0, {(2, 0): (2, 1), (3, 0): (3, 2)})
    near1 = hop(y1, {(1, 0): (2, 1)})
    far1 = hop(y1, {(1, 0): (3, 1)})
    y2 = finish((2, 1), given, product(((2, 1),), near1, held0))
    held1 = held0 + hop(product(((3, 1),), far1), {(3, 1): (3, 2)})
    near2 = hop(y2, {(2, 1): (3, 2)})
    y3 = finish((3, 2), given, product(((3, 2),), near2, held1))

    moved = hop(y1 + y2, {(1, 0): (1, 2), (2, 1): (2, 3)})
    back = jnp.where(z == 0, y0, moved)
    solved = rotated(in_order(back, swap_at(back, ((0, 1), (1, 2), (2, 3)))))

    y3 = hop(y3, {(3, 2): (3, 3)})
    y3_other = swap_at(y3, ((3, 3),))

    def last_tile(value, other, weights):
        return apply_rows(rotated(in_order(value, other)), weights)

    x3 = lax.cond(here((3, 3)), last_tile, lambda v, o, w: empty, y3, y3_other, rows)
    near3 = hop(x3, {(3, 3): (2, 3)})
    x2 = finish((2, 3), solved, product(((2, 3),), near3))
    far3 = hop(near3 + x3, {(3, 3): (0, 3), (2, 3): (1, 3)})
    held2 = hop(product(((0, 3), (1, 3)), far3), {(1, 3): (1, 2), (0, 3): (0, 1)})
    near4 = hop(x2, {(2, 3): (1, 2)})
    far4 = hop(x2, {(2, 3): (0, 2)})
    x1 = finish((1, 2), solved, product(((1, 2),), near4, held2))
    held3 = held2 + hop(product(((0, 2),), far4), {(0, 2): (0, 1)})
    near5 = hop(x1, {(1, 2): (0, 1)})
    x0 = finish((0, 1), solved, product(((0, 1),), near5, held3))

    found = x0 + x1 + x2 + x3
    share = herm_rows(found, basis_half)
    both = jnp.concatenate([found, share], 2)
    other = swap(both)
    share = share + other[:, :, half:]
    chosen = jnp.where((y < 2) == (c == 0), found, other[:, :, :half])
    mine = jnp.where(y % 2 == 0, chosen[:, :, :piece], chosen[:, :, piece:])
    message = jnp.concatenate([mine, share], 2)
    spreadout = jnp.broadcast_to(message[None], (SIDE * SIDE,) + message.shape)
    received = lax.all_to_all(spreadout, ("z", "x"), 0, 0)
    first = jnp.sum(received[:, :, :, piece:], 0)
    same = lax.dynamic_slice_in_dim(received[:, :, :, :piece], z * SIDE, SIDE, 0)
    own_rows = jnp.sum(same, 0)
    projected = own_rows - combine_rows(first, spread)
    coeffs = combine_rows(first, keep)
    return projected, jnp.swapaxes(coeffs, 1, 2)


def solution(mesh):
    split = Mesh(mesh.devices.reshape(SIDE, SIDE, SIDE, 2), AXES)
    row, col = ("z", "y"), ("x", "c")
    in_specs = (P(None, row, col), P(None, None, row), P(None, None, row), P(None, None, row), P(None, None, row))
    out_specs = (P(None, None, row), P())
    return jax.shard_map(local, mesh=split, in_specs=in_specs, out_specs=out_specs, check_vma=False)
```

```python
import jax
import jax.numpy as jnp
from jax import lax
from jax.sharding import Mesh, PartitionSpec as P

SIDE = 4
AXES = ("z", "y", "x", "c")
HIGH = lax.Precision.HIGH
HIGHEST = lax.Precision.HIGHEST


def dot_nt(left, right, precision):
    return lax.dot_general(left, right, (((1,), (1,)), ((), ())), precision=precision, preferred_element_type=jnp.float32)


def apply_rows(vectors, matrix, precision=HIGH):
    n = vectors.shape[1]
    both = jnp.concatenate([vectors[0], vectors[1]], 0)
    by_real = dot_nt(both, matrix[0], precision)
    by_imag = dot_nt(both, matrix[1], precision)
    return jnp.stack([by_real[:n] - by_imag[n:], by_real[n:] + by_imag[:n]])


def herm_rows(vectors, matrix, precision=HIGHEST):
    n = vectors.shape[1]
    both = jnp.concatenate([vectors[0], vectors[1]], 0)
    by_real = dot_nt(both, matrix[0], precision)
    by_imag = dot_nt(both, matrix[1], precision)
    return jnp.stack([by_real[:n] + by_imag[n:], by_real[n:] - by_imag[:n]])


def combine_rows(coeffs, matrix, precision=HIGHEST):
    n = coeffs.shape[1]
    both = jnp.concatenate([coeffs[0], coeffs[1]], 0)
    by_real = jnp.dot(both, matrix[0], precision=precision, preferred_element_type=jnp.float32)
    by_imag = jnp.dot(both, matrix[1], precision=precision, preferred_element_type=jnp.float32)
    return jnp.stack([by_real[:n] - by_imag[n:], by_real[n:] + by_imag[:n]])


def index_of(z, y, x, c):
    return ((z * SIDE + y) * SIDE + x) * 2 + c


def move(value, target):
    pairs = []
    for z in range(SIDE):
        for y in range(SIDE):
            for x in range(SIDE):
                for c in range(2):
                    there = target(z, y, x, c)
                    if there is not None:
                        pairs.append((index_of(z, y, x, c), index_of(*there)))
    return lax.ppermute(value, AXES, pairs)


def swap(value):
    return lax.ppermute(value, "c", [(0, 1), (1, 0)])


def turn_y(value, offset):
    return move(value, lambda z, y, x, c: (z, (y - offset) % SIDE, x, c))


def hop(value, routes):
    paired = dict(routes)
    paired.update({there: start for start, there in routes.items()})

    def target(z, y, x, c):
        there = paired.get((z, x))
        return (z, y, x, 1 - c) if there is None else (there[0], y, there[1], c)

    return move(value, target)


def local(factor, lower_inverse, upper_inverse, krylov_block, basis):
    z = lax.axis_index("z")
    y = lax.axis_index("y")
    x = lax.axis_index("x")
    c = lax.axis_index("c")
    piece = factor.shape[1]
    half = factor.shape[2]
    tile = 2 * half
    nvec = krylov_block.shape[1]
    nb = basis.shape[1]
    every = range(SIDE)

    def here(*places):
        found = jnp.zeros((), bool)
        for a, b in places:
            found = found | ((z == a) & (x == b))
        return found

    def rotated(value):
        return lax.dynamic_slice_in_dim(jnp.concatenate([value, value], 2), y * piece, tile, 2)

    def in_order(value, other):
        return jnp.concatenate([jnp.where(c == 0, value, other), jnp.where(c == 0, other, value)], 2)

    lower_half = lax.dynamic_slice_in_dim(lower_inverse, c * half, half, 1)
    upper_half = lax.dynamic_slice_in_dim(upper_inverse, c * half, half, 1)

    lead = apply_rows(krylov_block, lower_half)
    gram = herm_rows(basis, basis)
    lead = jnp.concatenate([lead, gram.reshape(2, nvec, half)], 2)
    lead_parts = [turn_y(lead, d) for d in (1, 3, 2)]

    inverse = jnp.where(x == (z + 3) % SIDE, lower_half, upper_half)
    left, right = factor[:, :, :piece], factor[:, :, piece:]
    packed = jnp.concatenate([left, right, inverse, krylov_block, basis], 1)
    pieces = [packed] + [turn_y(packed, d) for d in (1, 3, 2)]
    pieces = [pieces[0], pieces[1], pieces[3], pieces[2]]
    tall = jnp.concatenate([jnp.concatenate([p[:, :piece], p[:, piece:half]], 2) for p in pieces], 1)
    top = half + half
    rows = jnp.concatenate([p[:, half:top] for p in pieces], 2)
    given = jnp.concatenate([p[:, top:top + nvec] for p in pieces], 2)
    basis_all = jnp.stack([p[:, top + nvec:] for p in pieces])
    low = lax.dynamic_index_in_dim(basis_all, (2 * c - y) % SIDE, 0, False)
    high = lax.dynamic_index_in_dim(basis_all, (2 * c + 1 - y) % SIDE, 0, False)
    basis_half = jnp.concatenate([low, high], 2)

    lead = lead + lead_parts[0] + lead_parts[1] + lead_parts[2]
    y0 = lead[:, :, :half]
    gram = lead[:, :, half:].reshape(2, nb, nb)
    shifts = [[(i, (i + d) % SIDE) for i in every] for d in (1, 3, 2)]
    gram_parts = [lax.ppermute(gram, "z", s) for s in shifts]
    gram = gram + gram_parts[0] + gram_parts[1] + gram_parts[2]
    twice = jnp.stack([2.0 * jnp.eye(nb, dtype=jnp.float32), jnp.zeros((nb, nb), jnp.float32)])
    keep = twice - gram
    spread = combine_rows(keep, basis)
    y0, spread, keep = lax.optimization_barrier((y0, spread, keep))

    empty = jnp.zeros((2, nvec, half), jnp.float32)
    blank = jnp.zeros((2, nvec, tile), jnp.float32)

    def product(places, vectors):
        return lax.cond(here(*places), apply_rows, lambda v, w: blank, vectors, tall)

    def finish(place, right, acc):
        other = swap(acc)

        def run(right, acc, other, weights):
            return apply_rows(right - (acc + other), weights)

        return lax.cond(here(place), run, lambda r, a, o, w: empty, right, acc, other, rows)

    def widen(value):
        return jnp.concatenate([value, value], 2)

    acc0 = product(((1, 0), (2, 0), (3, 0)), hop(y0, {(0, 0): (1, 0), (0, 1): (2, 0), (0, 3): (3, 0)}))
    y1 = finish((1, 0), given, acc0)
    near1 = hop(y1, {(1, 0): (2, 1)})
    mixed1 = hop(jnp.where(z == 1, widen(y1), acc0), {(1, 0): (3, 1), (2, 0): (2, 1), (3, 0): (3, 2)})
    y2 = finish((2, 1), given, mixed1 + product(((2, 1),), near1))
    near2 = hop(y2, {(2, 1): (3, 2)})
    held1 = mixed1 + hop(product(((3, 1),), mixed1[:, :, :half]), {(3, 1): (3, 2)})
    y3 = finish((3, 2), given, held1 + product(((3, 2),), near2))

    moved = hop(y1 + y2 + y3, {(1, 0): (1, 2), (2, 1): (2, 3), (3, 2): (3, 3)})
    back = jnp.where(z == 0, y0, moved)
    solved = rotated(in_order(back, swap(back)))

    x3 = lax.cond(here((3, 3)), apply_rows, lambda v, w: empty, solved, rows)
    near3 = hop(x3, {(3, 3): (2, 3)})
    x2 = finish((2, 3), solved, product(((2, 3),), near3))
    far3 = hop(jnp.where(z == 3, x3, near3), {(3, 3): (0, 3), (2, 3): (1, 3)})
    near4 = hop(x2, {(2, 3): (1, 2)})
    side = product(((0, 3), (1, 3)), far3)
    mixed3 = hop(jnp.where(z == 2, widen(x2), side), {(2, 3): (0, 2), (1, 3): (1, 2), (0, 3): (0, 1)})
    x1 = finish((1, 2), solved, mixed3 + product(((1, 2),), near4))
    near5 = hop(x1, {(1, 2): (0, 1)})
    held3 = mixed3 + hop(product(((0, 2),), mixed3[:, :, :half]), {(0, 2): (0, 1)})
    x0 = finish((0, 1), solved, held3 + product(((0, 1),), near5))

    found = x0 + x1 + x2 + x3
    share = herm_rows(found, basis_half)
    both = jnp.concatenate([found, share], 2)
    other = swap(both)
    share = share + other[:, :, half:]
    chosen = jnp.where((y < 2) == (c == 0), found, other[:, :, :half])
    mine = jnp.where(y % 2 == 0, chosen[:, :, :piece], chosen[:, :, piece:])
    message = jnp.concatenate([mine, share], 2)
    spreadout = jnp.broadcast_to(message[None], (SIDE * SIDE,) + message.shape)
    received = lax.all_to_all(spreadout, ("z", "x"), 0, 0)
    first = jnp.sum(received[:, :, :, piece:], 0)
    same = lax.dynamic_slice_in_dim(received[:, :, :, :piece], z * SIDE, SIDE, 0)
    own_rows = jnp.sum(same, 0)
    projected = own_rows - combine_rows(first, spread)
    coeffs = combine_rows(first, keep)
    return projected, jnp.swapaxes(coeffs, 1, 2)


def solution(mesh):
    split = Mesh(mesh.devices.reshape(SIDE, SIDE, SIDE, 2), AXES)
    row, col = ("z", "y"), ("x", "c")
    in_specs = (P(None, row, col), P(None, None, row), P(None, None, row), P(None, None, row), P(None, None, row))
    out_specs = (P(None, None, row), P())
    return jax.shard_map(local, mesh=split, in_specs=in_specs, out_specs=out_specs, check_vma=False)
```

```python
import jax
import jax.numpy as jnp
from jax import lax
from jax.sharding import Mesh, PartitionSpec as P

SIDE = 4
AXES = ("z", "y", "x", "c")
HIGH = lax.Precision.HIGH
HIGHEST = lax.Precision.HIGHEST


def dot_nt(left, right, precision):
    return lax.dot_general(left, right, (((1,), (1,)), ((), ())), precision=precision, preferred_element_type=jnp.float32)


def apply_rows(vectors, matrix, precision=HIGH):
    n = vectors.shape[1]
    both = jnp.concatenate([vectors[0], vectors[1]], 0)
    by_real = dot_nt(both, matrix[0], precision)
    by_imag = dot_nt(both, matrix[1], precision)
    return jnp.stack([by_real[:n] - by_imag[n:], by_real[n:] + by_imag[:n]])


def herm_rows(vectors, matrix, precision=HIGHEST):
    n = vectors.shape[1]
    both = jnp.concatenate([vectors[0], vectors[1]], 0)
    by_real = dot_nt(both, matrix[0], precision)
    by_imag = dot_nt(both, matrix[1], precision)
    return jnp.stack([by_real[:n] + by_imag[n:], by_real[n:] - by_imag[:n]])


def combine_rows(coeffs, matrix, precision=HIGHEST):
    n = coeffs.shape[1]
    both = jnp.concatenate([coeffs[0], coeffs[1]], 0)
    by_real = jnp.dot(both, matrix[0], precision=precision, preferred_element_type=jnp.float32)
    by_imag = jnp.dot(both, matrix[1], precision=precision, preferred_element_type=jnp.float32)
    return jnp.stack([by_real[:n] - by_imag[n:], by_real[n:] + by_imag[:n]])


def index_of(z, y, x, c):
    return ((z * SIDE + y) * SIDE + x) * 2 + c


def move(value, target):
    pairs = []
    for z in range(SIDE):
        for y in range(SIDE):
            for x in range(SIDE):
                for c in range(2):
                    there = target(z, y, x, c)
                    if there is not None:
                        pairs.append((index_of(z, y, x, c), index_of(*there)))
    return lax.ppermute(value, AXES, pairs)


def swap(value):
    return lax.ppermute(value, "c", [(0, 1), (1, 0)])


def turn_y(value, offset):
    return move(value, lambda z, y, x, c: (z, (y - offset) % SIDE, x, c))


def hop(value, routes):
    paired = dict(routes)
    paired.update({there: start for start, there in routes.items()})

    def target(z, y, x, c):
        there = paired.get((z, x))
        return (z, y, x, 1 - c) if there is None else (there[0], y, there[1], c)

    return move(value, target)


def local(factor, lower_inverse, upper_inverse, krylov_block, basis):
    z = lax.axis_index("z")
    y = lax.axis_index("y")
    x = lax.axis_index("x")
    c = lax.axis_index("c")
    piece = factor.shape[1]
    half = factor.shape[2]
    tile = 2 * half
    nvec = krylov_block.shape[1]
    nb = basis.shape[1]
    every = range(SIDE)

    def here(*places):
        found = jnp.zeros((), bool)
        for a, b in places:
            found = found | ((z == a) & (x == b))
        return found

    def rotated(value):
        return lax.dynamic_slice_in_dim(jnp.concatenate([value, value], 2), y * piece, tile, 2)

    def in_order(value, other):
        return jnp.concatenate([jnp.where(c == 0, value, other), jnp.where(c == 0, other, value)], 2)

    lower_half = lax.dynamic_slice_in_dim(lower_inverse, c * half, half, 1)
    upper_half = lax.dynamic_slice_in_dim(upper_inverse, c * half, half, 1)

    inverse = jnp.where(x == (z + 3) % SIDE, lower_half, upper_half)
    left, right = factor[:, :, :piece], factor[:, :, piece:]
    packed = jnp.concatenate([left, right, inverse, krylov_block, basis], 1)
    packed, krylov_block, lower_half = lax.optimization_barrier((packed, krylov_block, lower_half))
    lead = apply_rows(krylov_block, lower_half)
    pieces = [packed] + [turn_y(packed, d) for d in (1, 3, 2)]
    pieces = [pieces[0], pieces[1], pieces[3], pieces[2]]
    tall = jnp.concatenate([jnp.concatenate([p[:, :piece], p[:, piece:half]], 2) for p in pieces], 1)
    top = half + half
    rows = jnp.concatenate([p[:, half:top] for p in pieces], 2)
    given = jnp.concatenate([p[:, top:top + nvec] for p in pieces], 2)
    basis_all = jnp.stack([p[:, top + nvec:] for p in pieces])
    low = lax.dynamic_index_in_dim(basis_all, (2 * c - y) % SIDE, 0, False)
    high = lax.dynamic_index_in_dim(basis_all, (2 * c + 1 - y) % SIDE, 0, False)
    basis_half = jnp.concatenate([low, high], 2)

    lead_parts = [turn_y(lead, d) for d in (1, 3, 2)]
    y0 = lead + lead_parts[0] + lead_parts[1] + lead_parts[2]
    plane = jnp.concatenate([basis_all[d] for d in every], 2)
    gram = herm_rows(plane, plane)

    empty = jnp.zeros((2, nvec, half), jnp.float32)
    blank = jnp.zeros((2, nvec, tile), jnp.float32)

    def product(places, vectors):
        return lax.cond(here(*places), apply_rows, lambda v, w: blank, vectors, tall)

    def finish(place, right, acc):
        other = swap(acc)

        def run(right, acc, other, weights):
            return apply_rows(right - (acc + other), weights)

        return lax.cond(here(place), run, lambda r, a, o, w: empty, right, acc, other, rows)

    def widen(value):
        return jnp.concatenate([value, value], 2)

    acc0 = product(((1, 0), (2, 0), (3, 0)), hop(y0, {(0, 0): (1, 0), (0, 1): (2, 0), (0, 3): (3, 0)}))
    y1 = finish((1, 0), given, acc0)
    near1 = hop(y1, {(1, 0): (2, 1)})
    early1 = hop(acc0, {(2, 0): (2, 1), (3, 0): (3, 2)})
    far1 = hop(y1, {(1, 0): (3, 1)})
    y2 = finish((2, 1), given, early1 + product(((2, 1),), near1))
    near2 = hop(y2, {(2, 1): (3, 2)})
    held1 = early1 + hop(product(((3, 1),), far1), {(3, 1): (3, 2)})
    y3 = finish((3, 2), given, held1 + product(((3, 2),), near2))

    moved = hop(y1 + y2 + y3, {(1, 0): (1, 2), (2, 1): (2, 3), (3, 2): (3, 3)})
    back = jnp.where(z == 0, y0, moved)
    solved = rotated(in_order(back, swap(back)))

    x3 = lax.cond(here((3, 3)), apply_rows, lambda v, w: empty, solved, rows)
    near3 = hop(x3, {(3, 3): (2, 3)})
    x2 = finish((2, 3), solved, product(((2, 3),), near3))
    far3 = hop(x3, {(3, 3): (1, 3)})
    side1 = hop(product(((1, 3),), far3), {(1, 3): (1, 2)})
    near4 = hop(x2 + x3, {(2, 3): (1, 2), (3, 3): (0, 3)})
    far4 = hop(x2, {(2, 3): (0, 2)})
    side0 = hop(product(((0, 3),), near4), {(0, 3): (0, 1)})
    x1 = finish((1, 2), solved, side1 + product(((1, 2),), near4))
    near5 = hop(x1, {(1, 2): (0, 1)})
    held3 = side0 + hop(product(((0, 2),), far4), {(0, 2): (0, 1)})
    x0 = finish((0, 1), solved, held3 + product(((0, 1),), near5))

    found = x0 + x1 + x2 + x3
    share = herm_rows(found, basis_half)
    both = jnp.concatenate([found, share], 2)
    other = swap(both)
    share = share + other[:, :, half:]
    chosen = jnp.where((y < 2) == (c == 0), found, other[:, :, :half])
    mine = jnp.where(y % 2 == 0, chosen[:, :, :piece], chosen[:, :, piece:])
    message = jnp.concatenate([mine, share], 2)
    shifts = [[(i, (i + d) % SIDE) for i in every] for d in (1, 3, 2)]
    across = [lax.ppermute(message, "x", s) for s in shifts]
    message = message + across[0] + across[1] + across[2]
    own_rows = message[:, :, :piece]
    sums = jnp.concatenate([message[:, :, piece:], gram], 1)
    planes = [lax.ppermute(sums, "z", s) for s in shifts]
    sums = sums + planes[0] + planes[1] + planes[2]
    first, gram = sums[:, :nvec], sums[:, nvec:]
    coeffs = 2.0 * first - combine_rows(first, gram)
    projected = own_rows - combine_rows(coeffs, basis)
    return projected, jnp.swapaxes(coeffs, 1, 2)


def solution(mesh):
    split = Mesh(mesh.devices.reshape(SIDE, SIDE, SIDE, 2), AXES)
    row, col = ("z", "y"), ("x", "c")
    in_specs = (P(None, row, col), P(None, None, row), P(None, None, row), P(None, None, row), P(None, None, row))
    out_specs = (P(None, None, row), P())
    return jax.shard_map(local, mesh=split, in_specs=in_specs, out_specs=out_specs, check_vma=False)
```

```python
import jax
import jax.numpy as jnp
from jax import lax
from jax.sharding import Mesh, PartitionSpec as P

SIDE = 4
AXES = ("z", "y", "x", "c")
HIGH = lax.Precision.HIGH
HIGHEST = lax.Precision.HIGHEST


def dot_nt(left, right, precision):
    return lax.dot_general(left, right, (((1,), (1,)), ((), ())), precision=precision, preferred_element_type=jnp.float32)


def apply_rows(vectors, matrix, precision=HIGH):
    n = vectors.shape[1]
    both = jnp.concatenate([vectors[0], vectors[1]], 0)
    by_real = dot_nt(both, matrix[0], precision)
    by_imag = dot_nt(both, matrix[1], precision)
    return jnp.stack([by_real[:n] - by_imag[n:], by_real[n:] + by_imag[:n]])


def herm_rows(vectors, matrix, precision=HIGHEST):
    n = vectors.shape[1]
    both = jnp.concatenate([vectors[0], vectors[1]], 0)
    by_real = dot_nt(both, matrix[0], precision)
    by_imag = dot_nt(both, matrix[1], precision)
    return jnp.stack([by_real[:n] + by_imag[n:], by_real[n:] - by_imag[:n]])


def combine_rows(coeffs, matrix, precision=HIGHEST):
    n = coeffs.shape[1]
    both = jnp.concatenate([coeffs[0], coeffs[1]], 0)
    by_real = jnp.dot(both, matrix[0], precision=precision, preferred_element_type=jnp.float32)
    by_imag = jnp.dot(both, matrix[1], precision=precision, preferred_element_type=jnp.float32)
    return jnp.stack([by_real[:n] - by_imag[n:], by_real[n:] + by_imag[:n]])


def index_of(z, y, x, c):
    return ((z * SIDE + y) * SIDE + x) * 2 + c


def move(value, target):
    pairs = []
    for z in range(SIDE):
        for y in range(SIDE):
            for x in range(SIDE):
                for c in range(2):
                    there = target(z, y, x, c)
                    if there is not None:
                        pairs.append((index_of(z, y, x, c), index_of(*there)))
    return lax.ppermute(value, AXES, pairs)


def swap(value):
    return lax.ppermute(value, "c", [(0, 1), (1, 0)])


def turn_y(value, offset):
    return move(value, lambda z, y, x, c: (z, (y - offset) % SIDE, x, c))


def hop(value, routes):
    paired = dict(routes)
    paired.update({there: start for start, there in routes.items()})

    def target(z, y, x, c):
        there = paired.get((z, x))
        return (z, y, x, 1 - c) if there is None else (there[0], y, there[1], c)

    return move(value, target)


def local(factor, lower_inverse, upper_inverse, krylov_block, basis):
    z = lax.axis_index("z")
    y = lax.axis_index("y")
    x = lax.axis_index("x")
    c = lax.axis_index("c")
    piece = factor.shape[1]
    half = factor.shape[2]
    tile = 2 * half
    nvec = krylov_block.shape[1]
    nb = basis.shape[1]
    every = range(SIDE)

    def here(*places):
        found = jnp.zeros((), bool)
        for a, b in places:
            found = found | ((z == a) & (x == b))
        return found

    def rotated(value):
        return lax.dynamic_slice_in_dim(jnp.concatenate([value, value], 2), y * piece, tile, 2)

    def in_order(value, other):
        return jnp.concatenate([jnp.where(c == 0, value, other), jnp.where(c == 0, other, value)], 2)

    lower_half = lax.dynamic_slice_in_dim(lower_inverse, c * half, half, 1)
    upper_half = lax.dynamic_slice_in_dim(upper_inverse, c * half, half, 1)

    inverse = jnp.where(jnp.where(z == 0, x != 1, x == z - 1), lower_half, upper_half)
    left, right = factor[:, :, :piece], factor[:, :, piece:]
    packed = jnp.concatenate([left, right, inverse, krylov_block, basis], 1)
    pieces = [packed] + [turn_y(packed, d) for d in (1, 3, 2)]
    pieces = [pieces[0], pieces[1], pieces[3], pieces[2]]
    tall = jnp.concatenate([jnp.concatenate([p[:, :piece], p[:, piece:half]], 2) for p in pieces], 1)
    top = half + half
    rows = jnp.concatenate([p[:, half:top] for p in pieces], 2)
    given = jnp.concatenate([p[:, top:top + nvec] for p in pieces], 2)
    basis_all = jnp.stack([p[:, top + nvec:] for p in pieces])
    low = lax.dynamic_index_in_dim(basis_all, (2 * c - y) % SIDE, 0, False)
    high = lax.dynamic_index_in_dim(basis_all, (2 * c + 1 - y) % SIDE, 0, False)
    basis_half = jnp.concatenate([low, high], 2)

    plane = jnp.concatenate([basis_all[d] for d in every], 2)
    gram = herm_rows(plane, plane)

    empty = jnp.zeros((2, nvec, half), jnp.float32)
    small = jnp.zeros((2, nvec, nb), jnp.float32)
    blank = jnp.zeros((2, nvec, tile), jnp.float32)

    def product(places, vectors):
        return lax.cond(here(*places), apply_rows, lambda v, w: blank, vectors, tall)

    def finish(place, right, acc):
        other = swap(acc)

        def run(right, acc, other, weights):
            return apply_rows(right - (acc + other), weights)

        return lax.cond(here(place), run, lambda r, a, o, w: empty, right, acc, other, rows)

    def share(value, place):
        part = lax.cond(here(place), herm_rows, lambda v, w: small, value, basis_half)
        return jnp.concatenate([part, gram], 1)

    starts = ((0, 0), (0, 2), (0, 3))
    y0 = lax.cond(here(*starts), apply_rows, lambda v, w: empty, given, rows)
    arrived = hop(y0, {(0, 0): (1, 0), (0, 2): (2, 0), (0, 3): (3, 0)})
    arrived, gram = lax.optimization_barrier((arrived, gram))
    acc0 = product(((1, 0), (2, 0), (3, 0)), arrived)
    y1 = finish((1, 0), given, acc0)
    near1 = hop(y1, {(1, 0): (2, 1)})
    early1 = hop(acc0, {(2, 0): (2, 1), (3, 0): (3, 2)})
    far1 = hop(y1, {(1, 0): (3, 1)})
    y2 = finish((2, 1), given, early1 + product(((2, 1),), near1))
    near2 = hop(y2, {(2, 1): (3, 2)})
    held1 = early1 + hop(product(((3, 1),), far1), {(3, 1): (3, 2)})
    y3 = finish((3, 2), given, held1 + product(((3, 2),), near2))

    back = hop(y0 + y1 + y2 + y3, {(0, 0): (0, 1), (1, 0): (1, 2), (2, 1): (2, 3), (3, 2): (3, 3)})
    solved = rotated(in_order(back, swap(back)))

    x3 = lax.cond(here((3, 3)), apply_rows, lambda v, w: empty, solved, rows)
    near3 = hop(x3, {(3, 3): (2, 3)})
    sent3 = hop(share(x3, (3, 3)), {(3, 3): (0, 1)})
    x2 = finish((2, 3), solved, product(((2, 3),), near3))
    far3 = hop(x3, {(3, 3): (1, 3)})
    side1 = hop(product(((1, 3),), far3), {(1, 3): (1, 2)})
    near4 = hop(x2 + x3, {(2, 3): (1, 2), (3, 3): (0, 3)})
    far4 = hop(x2, {(2, 3): (0, 2)})
    sent2 = hop(share(x2, (2, 3)), {(2, 3): (0, 1)})
    side0 = hop(product(((0, 3),), near4), {(0, 3): (0, 1)})
    x1 = finish((1, 2), solved, side1 + product(((1, 2),), near4))
    near5 = hop(x1, {(1, 2): (0, 1)})
    sent1 = hop(share(x1, (1, 2)), {(1, 2): (0, 1)})
    held3 = side0 + hop(product(((0, 2),), far4), {(0, 2): (0, 1)})
    x0 = finish((0, 1), solved, held3 + product(((0, 1),), near5))

    found = x0 + x1 + x2 + x3
    sums = share(x0, (0, 1)) + (sent1 + sent2 + sent3)
    both = jnp.concatenate([found, sums[:, :nvec]], 2)
    other = swap(both)
    first = sums[:, :nvec] + other[:, :, half:]
    coeffs = 2.0 * first - combine_rows(first, sums[:, nvec:])
    chosen = jnp.where((y < 2) == (c == 0), found, other[:, :, :half])
    mine = jnp.where(y % 2 == 0, chosen[:, :, :piece], chosen[:, :, piece:])
    message = jnp.concatenate([mine, coeffs], 2)
    columns = (1, 2, 3, 3)
    column = jnp.where(z == 0, 1, jnp.where(z == 1, 2, 3))
    for d in (1, 3, 2):
        landed = hop(message, {(a, columns[a]): (a, (columns[a] + d) % SIDE) for a in every})
        if d == 1:
            chain = jnp.where(x == column, message, landed)
        else:
            chain = jnp.where(x == (column + d) % SIDE, landed, chain)
    own_rows = chain[:, :, :piece]
    coeffs = chain[:, :, piece:]
    total = coeffs
    for a in (1, 3, 2):
        landed = hop(coeffs, {(0, b): (a, b) for b in every})
        total = jnp.where(z == a, landed, total)
    projected = own_rows - combine_rows(total, basis)
    return projected, jnp.swapaxes(total, 1, 2)


def solution(mesh):
    split = Mesh(mesh.devices.reshape(SIDE, SIDE, SIDE, 2), AXES)
    row, col = ("z", "y"), ("x", "c")
    in_specs = (P(None, row, col), P(None, None, row), P(None, None, row), P(None, None, row), P(None, None, row))
    out_specs = (P(None, None, row), P())
    return jax.shard_map(local, mesh=split, in_specs=in_specs, out_specs=out_specs, check_vma=False)
```

```python
import jax
import jax.numpy as jnp
from jax import lax
from jax.sharding import Mesh, PartitionSpec as P

SIDE = 4
AXES = ("z", "y", "x", "c")
HIGH = lax.Precision.HIGH
HIGHEST = lax.Precision.HIGHEST


def dot_nt(left, right, precision):
    return lax.dot_general(left, right, (((1,), (1,)), ((), ())), precision=precision, preferred_element_type=jnp.float32)


def apply_rows(vectors, matrix, precision=HIGH):
    n = vectors.shape[1]
    both = jnp.concatenate([vectors[0], vectors[1]], 0)
    by_real = dot_nt(both, matrix[0], precision)
    by_imag = dot_nt(both, matrix[1], precision)
    return jnp.stack([by_real[:n] - by_imag[n:], by_real[n:] + by_imag[:n]])


def herm_rows(vectors, matrix, precision=HIGHEST):
    n = vectors.shape[1]
    both = jnp.concatenate([vectors[0], vectors[1]], 0)
    by_real = dot_nt(both, matrix[0], precision)
    by_imag = dot_nt(both, matrix[1], precision)
    return jnp.stack([by_real[:n] + by_imag[n:], by_real[n:] - by_imag[:n]])


def combine_rows(coeffs, matrix, precision=HIGHEST):
    n = coeffs.shape[1]
    both = jnp.concatenate([coeffs[0], coeffs[1]], 0)
    by_real = jnp.dot(both, matrix[0], precision=precision, preferred_element_type=jnp.float32)
    by_imag = jnp.dot(both, matrix[1], precision=precision, preferred_element_type=jnp.float32)
    return jnp.stack([by_real[:n] - by_imag[n:], by_real[n:] + by_imag[:n]])


def index_of(z, y, x, c):
    return ((z * SIDE + y) * SIDE + x) * 2 + c


def move(value, target):
    pairs = []
    for z in range(SIDE):
        for y in range(SIDE):
            for x in range(SIDE):
                for c in range(2):
                    there = target(z, y, x, c)
                    if there is not None:
                        pairs.append((index_of(z, y, x, c), index_of(*there)))
    return lax.ppermute(value, AXES, pairs)


def swap(value):
    return lax.ppermute(value, "c", [(0, 1), (1, 0)])


def turn_y(value, offset):
    return move(value, lambda z, y, x, c: (z, (y - offset) % SIDE, x, c))


def hop(value, routes, idle=()):
    paired = dict(routes)
    spare = dict(zip(routes.values(), idle))
    for start, there in routes.items():
        if there in spare:
            paired[there] = spare[there]
            paired[spare[there]] = start
        else:
            paired[there] = start

    def target(z, y, x, c):
        there = paired.get((z, x))
        return (z, y, x, 1 - c) if there is None else (there[0], y, there[1], c)

    return move(value, target)


def local(factor, lower_inverse, upper_inverse, krylov_block, basis):
    z = lax.axis_index("z")
    y = lax.axis_index("y")
    x = lax.axis_index("x")
    c = lax.axis_index("c")
    piece = factor.shape[1]
    half = factor.shape[2]
    tile = 2 * half
    nvec = krylov_block.shape[1]
    nb = basis.shape[1]
    every = range(SIDE)

    def here(*places):
        found = jnp.zeros((), bool)
        for a, b in places:
            found = found | ((z == a) & (x == b))
        return found

    def rotated(value):
        return lax.dynamic_slice_in_dim(jnp.concatenate([value, value], 2), y * piece, tile, 2)

    def in_order(value, other):
        return jnp.concatenate([jnp.where(c == 0, value, other), jnp.where(c == 0, other, value)], 2)

    lower_half = lax.dynamic_slice_in_dim(lower_inverse, c * half, half, 1)
    upper_half = lax.dynamic_slice_in_dim(upper_inverse, c * half, half, 1)

    inverse = jnp.where(jnp.where(z == 0, x != 1, x == z - 1), lower_half, upper_half)
    left, right = factor[:, :, :piece], factor[:, :, piece:]
    packed = jnp.concatenate([left, right, inverse, krylov_block, basis], 1)
    pieces = [packed] + [turn_y(packed, d) for d in (1, 3, 2)]
    pieces = [pieces[0], pieces[1], pieces[3], pieces[2]]
    tall = jnp.concatenate([jnp.concatenate([p[:, :piece], p[:, piece:half]], 2) for p in pieces], 1)
    top = half + half
    rows = jnp.concatenate([p[:, half:top] for p in pieces], 2)
    given = jnp.concatenate([p[:, top:top + nvec] for p in pieces], 2)
    basis_all = jnp.stack([p[:, top + nvec:] for p in pieces])
    low = lax.dynamic_index_in_dim(basis_all, (2 * c - y) % SIDE, 0, False)
    high = lax.dynamic_index_in_dim(basis_all, (2 * c + 1 - y) % SIDE, 0, False)
    basis_half = jnp.concatenate([low, high], 2)

    plane = jnp.concatenate([basis_all[d] for d in every], 2)
    gram = herm_rows(plane, plane)

    empty = jnp.zeros((2, nvec, half), jnp.float32)
    small = jnp.zeros((2, nvec, nb), jnp.float32)
    blank = jnp.zeros((2, nvec, tile), jnp.float32)

    def product(places, vectors):
        return lax.cond(here(*places), apply_rows, lambda v, w: blank, vectors, tall)

    def finish(place, right, acc):
        other = swap(acc)

        def run(right, acc, other, weights):
            return apply_rows(right - (acc + other), weights)

        return lax.cond(here(place), run, lambda r, a, o, w: empty, right, acc, other, rows)

    def after(value, other):
        return lax.optimization_barrier((value, other))[0]

    def share(value, place):
        part = lax.cond(here(place), herm_rows, lambda v, w: small, value, basis_half)
        return jnp.concatenate([part, gram], 1)

    starts = ((0, 0), (0, 2), (0, 3))
    y0 = lax.cond(here(*starts), apply_rows, lambda v, w: empty, given, rows)
    arrived = hop(y0, {(0, 0): (1, 0), (0, 2): (2, 0), (0, 3): (3, 0)})
    arrived, gram = lax.optimization_barrier((arrived, gram))
    acc0 = product(((1, 0),), arrived)
    y1 = finish((1, 0), given, acc0)
    near1 = hop(y1, {(1, 0): (2, 1)})
    far1 = hop(y1, {(1, 0): (3, 1)})
    near1, far1 = lax.optimization_barrier((near1, far1))
    early1 = hop(product(((2, 0), (3, 0)), after(arrived, y1)), {(2, 0): (2, 1), (3, 0): (3, 2)}, ((2, 2), (1, 1)))
    y2 = finish((2, 1), given, early1 + product(((2, 1),), near1))
    near2 = hop(y2, {(2, 1): (3, 2)})
    held1 = early1 + hop(product(((3, 1),), after(far1, y2)), {(3, 1): (3, 2)}, ((2, 2),))
    y3 = finish((3, 2), given, held1 + product(((3, 2),), near2))

    sent1 = hop(after(gram, y1), {(1, 2): (0, 1)})
    y3, sent1 = lax.optimization_barrier((y3, sent1))
    back = hop(y0 + y1 + y2 + y3, {(0, 0): (0, 1), (1, 0): (1, 2), (2, 1): (2, 3), (3, 2): (3, 3)})
    solved = rotated(in_order(back, swap(back)))

    x3 = lax.cond(here((3, 3)), apply_rows, lambda v, w: empty, solved, rows)
    near3 = hop(x3, {(3, 3): (2, 3)})
    far3 = hop(x3, {(3, 3): (1, 3)})
    x2 = finish((2, 3), solved, product(((2, 3),), near3))
    near4 = hop(x2 + x3, {(2, 3): (1, 2), (3, 3): (0, 3)})
    side1 = hop(product(((1, 3),), after(far3, x2)), {(1, 3): (1, 2)}, ((1, 1),))
    far4 = hop(x2, {(2, 3): (0, 2)})
    sent3 = hop(after(share(x3, (3, 3)), x2), {(3, 3): (0, 1)}, ((0, 0),))
    sent2 = hop(share(x2, (2, 3)), {(2, 3): (0, 1)}, ((1, 1),))
    x1 = finish((1, 2), solved, side1 + product(((1, 2),), near4))
    x1, sent2, sent3 = lax.optimization_barrier((x1, sent2, sent3))
    part1 = lax.cond(here((1, 2)), herm_rows, lambda v, w: small, x1, basis_half)
    near5 = hop(jnp.concatenate([x1, part1], 2), {(1, 2): (0, 1)})
    part1 = near5[:, :, half:]
    side0 = hop(after(product(((0, 3),), near4), x1), {(0, 3): (0, 1)}, ((0, 0),))
    held3 = side0 + hop(after(product(((0, 2),), far4), x1), {(0, 2): (0, 1)}, ((1, 1),))
    sent = jnp.concatenate([part1 + sent2[:, :nvec] + sent3[:, :nvec], sent1 + sent2[:, nvec:] + sent3[:, nvec:]], 1)
    near5 = near5[:, :, :half]
    x0 = finish((0, 1), solved, held3 + product(((0, 1),), near5))

    found = x0 + x1 + x2 + x3
    sums = share(x0, (0, 1)) + sent
    both = jnp.concatenate([found, sums[:, :nvec]], 2)
    other = swap(both)
    first = sums[:, :nvec] + other[:, :, half:]
    coeffs = 2.0 * first - combine_rows(first, sums[:, nvec:])
    chosen = jnp.where((y < 2) == (c == 0), found, other[:, :, :half])
    mine = jnp.where(y % 2 == 0, chosen[:, :, :piece], chosen[:, :, piece:])
    message = jnp.concatenate([mine, coeffs], 2)
    columns = (1, 2, 3, 3)
    column = jnp.where(z == 0, 1, jnp.where(z == 1, 2, 3))
    for d in (1, 3, 2):
        landed = hop(message, {(a, columns[a]): (a, (columns[a] + d) % SIDE) for a in every})
        if d == 1:
            chain = jnp.where(x == column, message, landed)
        else:
            chain = jnp.where(x == (column + d) % SIDE, landed, chain)
    own_rows = chain[:, :, :piece]
    coeffs = chain[:, :, piece:]
    total = coeffs
    for a in (1, 3, 2):
        landed = hop(coeffs, {(0, b): (a, b) for b in every})
        total = jnp.where(z == a, landed, total)
    projected = own_rows - combine_rows(total, basis)
    return projected, jnp.swapaxes(total, 1, 2)


def solution(mesh):
    split = Mesh(mesh.devices.reshape(SIDE, SIDE, SIDE, 2), AXES)
    row, col = ("z", "y"), ("x", "c")
    in_specs = (P(None, row, col), P(None, None, row), P(None, None, row), P(None, None, row), P(None, None, row))
    out_specs = (P(None, None, row), P())
    return jax.shard_map(local, mesh=split, in_specs=in_specs, out_specs=out_specs, check_vma=False)
```

```python
import jax
import jax.numpy as jnp
from jax import lax
from jax.sharding import Mesh, PartitionSpec as P

SIDE = 4
AXES = ("z", "y", "x", "c")
HIGH = lax.Precision.HIGH
HIGHEST = lax.Precision.HIGHEST


def dot_nt(left, right, precision):
    return lax.dot_general(left, right, (((1,), (1,)), ((), ())), precision=precision, preferred_element_type=jnp.float32)


def apply_rows(vectors, matrix, precision=HIGH):
    n = vectors.shape[1]
    both = jnp.concatenate([vectors[0], vectors[1]], 0)
    by_real = dot_nt(both, matrix[0], precision)
    by_imag = dot_nt(both, matrix[1], precision)
    return jnp.stack([by_real[:n] - by_imag[n:], by_real[n:] + by_imag[:n]])


def herm_rows(vectors, matrix, precision=HIGHEST):
    n = vectors.shape[1]
    both = jnp.concatenate([vectors[0], vectors[1]], 0)
    by_real = dot_nt(both, matrix[0], precision)
    by_imag = dot_nt(both, matrix[1], precision)
    return jnp.stack([by_real[:n] + by_imag[n:], by_real[n:] - by_imag[:n]])


def combine_rows(coeffs, matrix, precision=HIGHEST):
    n = coeffs.shape[1]
    both = jnp.concatenate([coeffs[0], coeffs[1]], 0)
    by_real = jnp.dot(both, matrix[0], precision=precision, preferred_element_type=jnp.float32)
    by_imag = jnp.dot(both, matrix[1], precision=precision, preferred_element_type=jnp.float32)
    return jnp.stack([by_real[:n] - by_imag[n:], by_real[n:] + by_imag[:n]])


def index_of(z, y, x, c):
    return ((z * SIDE + y) * SIDE + x) * 2 + c


def move(value, target):
    pairs = []
    for z in range(SIDE):
        for y in range(SIDE):
            for x in range(SIDE):
                for c in range(2):
                    there = target(z, y, x, c)
                    if there is not None:
                        pairs.append((index_of(z, y, x, c), index_of(*there)))
    return lax.ppermute(value, AXES, pairs)


def swap(value):
    return lax.ppermute(value, "c", [(0, 1), (1, 0)])


def turn_y(value, offset):
    return move(value, lambda z, y, x, c: (z, (y - offset) % SIDE, x, c))


def hop(value, routes, idle=()):
    paired = dict(routes)
    spare = dict(zip(routes.values(), idle))
    for start, there in routes.items():
        if there in spare:
            paired[there] = spare[there]
            paired[spare[there]] = start
        else:
            paired[there] = start

    def target(z, y, x, c):
        there = paired.get((z, x))
        return (z, y, x, 1 - c) if there is None else (there[0], y, there[1], c)

    return move(value, target)


def local(factor, lower_inverse, upper_inverse, krylov_block, basis):
    z = lax.axis_index("z")
    y = lax.axis_index("y")
    x = lax.axis_index("x")
    c = lax.axis_index("c")
    piece = factor.shape[1]
    half = factor.shape[2]
    tile = 2 * half
    nvec = krylov_block.shape[1]
    nb = basis.shape[1]
    every = range(SIDE)

    def here(*places):
        found = jnp.zeros((), bool)
        for a, b in places:
            found = found | ((z == a) & (x == b))
        return found

    def rotated(value):
        return lax.dynamic_slice_in_dim(jnp.concatenate([value, value], 2), y * piece, tile, 2)

    def in_order(value, other):
        return jnp.concatenate([jnp.where(c == 0, value, other), jnp.where(c == 0, other, value)], 2)

    lower_half = lax.dynamic_slice_in_dim(lower_inverse, c * half, half, 1)
    upper_half = lax.dynamic_slice_in_dim(upper_inverse, c * half, half, 1)

    inverse = jnp.where(jnp.where(z == 0, x != 1, x == z - 1), lower_half, upper_half)
    left, right = factor[:, :, :piece], factor[:, :, piece:]
    packed = jnp.concatenate([left, right, inverse, krylov_block, basis], 1)
    packed, krylov_block, lower_half = lax.optimization_barrier((packed, krylov_block, lower_half))
    lead = jnp.concatenate([apply_rows(krylov_block, lower_half), herm_rows(basis, basis).reshape(2, nvec, half)], 2)
    lead = lead + move(lead, lambda z, y, x, c: (z, y ^ 1, x, c))
    lead = lead + move(lead, lambda z, y, x, c: (z, 3 - y, x, c))
    gram = lead[:, :, half:].reshape(2, nb, nb)
    pieces = [packed] + [turn_y(packed, d) for d in (1, 3, 2)]
    pieces = [pieces[0], pieces[1], pieces[3], pieces[2]]
    tall = jnp.concatenate([jnp.concatenate([p[:, :piece], p[:, piece:half]], 2) for p in pieces], 1)
    top = half + half
    rows = jnp.concatenate([p[:, half:top] for p in pieces], 2)
    given = jnp.concatenate([p[:, top:top + nvec] for p in pieces], 2)
    basis_all = jnp.stack([p[:, top + nvec:] for p in pieces])
    low = lax.dynamic_index_in_dim(basis_all, (2 * c - y) % SIDE, 0, False)
    high = lax.dynamic_index_in_dim(basis_all, (2 * c + 1 - y) % SIDE, 0, False)
    basis_half = jnp.concatenate([low, high], 2)

    empty = jnp.zeros((2, nvec, half), jnp.float32)
    small = jnp.zeros((2, nvec, nb), jnp.float32)
    blank = jnp.zeros((2, nvec, tile), jnp.float32)

    def product(places, vectors):
        return lax.cond(here(*places), apply_rows, lambda v, w: blank, vectors, tall)

    def finish(place, right, acc):
        other = swap(acc)

        def run(right, acc, other, weights):
            return apply_rows(right - (acc + other), weights)

        return lax.cond(here(place), run, lambda r, a, o, w: empty, right, acc, other, rows)

    def after(value, other):
        return lax.optimization_barrier((value, other))[0]

    def share(value, place):
        part = lax.cond(here(place), herm_rows, lambda v, w: small, value, basis_half)
        return jnp.concatenate([part, gram], 1)

    starts = ((0, 0), (0, 2), (0, 3))
    arrived = hop(lead[:, :, :half], {(0, 0): (1, 0), (0, 2): (2, 0), (0, 3): (3, 0)})
    y0 = jnp.where(here(*starts), lead[:, :, :half], 0.0)
    acc0 = product(((1, 0),), arrived)
    y1 = finish((1, 0), given, acc0)
    near1 = hop(y1, {(1, 0): (2, 1)})
    far1 = hop(y1, {(1, 0): (3, 1)})
    near1, far1 = lax.optimization_barrier((near1, far1))
    early1 = hop(product(((2, 0), (3, 0)), after(arrived, y1)), {(2, 0): (2, 1), (3, 0): (3, 2)}, ((2, 2), (1, 1)))
    y2 = finish((2, 1), given, early1 + product(((2, 1),), near1))
    near2 = hop(y2, {(2, 1): (3, 2)})
    held1 = early1 + hop(product(((3, 1),), after(far1, y2)), {(3, 1): (3, 2)}, ((2, 2),))
    y3 = finish((3, 2), given, held1 + product(((3, 2),), near2))

    sent1 = hop(after(gram, y1), {(1, 2): (0, 1)})
    y3, sent1 = lax.optimization_barrier((y3, sent1))
    back = hop(y0 + y1 + y2 + y3, {(0, 0): (0, 1), (1, 0): (1, 2), (2, 1): (2, 3), (3, 2): (3, 3)})
    solved = rotated(in_order(back, swap(back)))

    x3 = lax.cond(here((3, 3)), apply_rows, lambda v, w: empty, solved, rows)
    near3 = hop(x3, {(3, 3): (2, 3)})
    far3 = hop(x3, {(3, 3): (1, 3)})
    x2 = finish((2, 3), solved, product(((2, 3),), near3))
    near4 = hop(x2 + x3, {(2, 3): (1, 2), (3, 3): (0, 3)})
    side1 = hop(product(((1, 3),), after(far3, x2)), {(1, 3): (1, 2)}, ((1, 1),))
    far4 = hop(x2, {(2, 3): (0, 2)})
    share3, share2 = share(x3, (3, 3)), share(x2, (2, 3))
    x1 = finish((1, 2), solved, side1 + product(((1, 2),), near4))
    sent3 = hop(after(share3, x1), {(3, 3): (0, 1)}, ((0, 0),))
    sent2 = hop(after(share2, x1), {(2, 3): (0, 1)}, ((1, 1),))
    part1 = lax.cond(here((1, 2)), herm_rows, lambda v, w: small, x1, basis_half)
    near5 = hop(jnp.concatenate([x1, part1], 2), {(1, 2): (0, 1)})
    part1 = near5[:, :, half:]
    side0 = hop(after(product(((0, 3),), near4), x1), {(0, 3): (0, 1)}, ((0, 0),))
    held3 = side0 + hop(after(product(((0, 2),), far4), x1), {(0, 2): (0, 1)}, ((1, 1),))
    sent = jnp.concatenate([part1 + sent2[:, :nvec] + sent3[:, :nvec], sent1 + sent2[:, nvec:] + sent3[:, nvec:]], 1)
    near5 = near5[:, :, :half]
    x0 = finish((0, 1), solved, held3 + product(((0, 1),), near5))

    found = x0 + x1 + x2 + x3
    sums = share(x0, (0, 1)) + sent
    both = jnp.concatenate([found, sums[:, :nvec]], 2)
    other = swap(both)
    first = sums[:, :nvec] + other[:, :, half:]
    coeffs = 2.0 * first - combine_rows(first, sums[:, nvec:])
    sure = coeffs
    chosen = jnp.where((y < 2) == (c == 0), found, other[:, :, :half])
    mine = jnp.where(y % 2 == 0, chosen[:, :, :piece], chosen[:, :, piece:])
    message = jnp.concatenate([mine, coeffs], 2)
    columns = (1, 2, 3, 3)
    column = jnp.where(z == 0, 1, jnp.where(z == 1, 2, 3))
    for d in (1, 3, 2):
        landed = hop(message, {(a, columns[a]): (a, (columns[a] + d) % SIDE) for a in every})
        if d == 1:
            chain = jnp.where(x == column, message, landed)
        else:
            chain = jnp.where(x == (column + d) % SIDE, landed, chain)
    own_rows = chain[:, :, :piece]
    coeffs = chain[:, :, piece:]
    total = coeffs
    for a in (1, 3, 2):
        landed = hop(sure, {(0, 1): (a, 1)})
        total = jnp.where((z == a) & (x == 1), landed, total)
    relay = total
    for d in (1, 3, 2):
        landed = hop(relay, {(a, 1): (a, (1 + d) % SIDE) for a in (1, 2, 3)})
        total = jnp.where((z > 0) & (x == (1 + d) % SIDE), landed, total)
    projected = own_rows - combine_rows(total, basis)
    return projected, jnp.swapaxes(total, 1, 2)


def solution(mesh):
    split = Mesh(mesh.devices.reshape(SIDE, SIDE, SIDE, 2), AXES)
    row, col = ("z", "y"), ("x", "c")
    in_specs = (P(None, row, col), P(None, None, row), P(None, None, row), P(None, None, row), P(None, None, row))
    out_specs = (P(None, None, row), P())
    return jax.shard_map(local, mesh=split, in_specs=in_specs, out_specs=out_specs, check_vma=False)
```

```python
import jax
import jax.numpy as jnp
from jax import lax
from jax.sharding import Mesh, PartitionSpec as P

SIDE = 4
AXES = ("z", "y", "x", "c")
HIGH = lax.Precision.HIGH
HIGHEST = lax.Precision.HIGHEST


def dot_nt(left, right, precision):
    return lax.dot_general(left, right, (((1,), (1,)), ((), ())), precision=precision, preferred_element_type=jnp.float32)


def apply_rows(vectors, matrix, precision=HIGH):
    n = vectors.shape[1]
    both = jnp.concatenate([vectors[0], vectors[1]], 0)
    by_real = dot_nt(both, matrix[0], precision)
    by_imag = dot_nt(both, matrix[1], precision)
    return jnp.stack([by_real[:n] - by_imag[n:], by_real[n:] + by_imag[:n]])


def herm_rows(vectors, matrix, precision=HIGHEST):
    n = vectors.shape[1]
    both = jnp.concatenate([vectors[0], vectors[1]], 0)
    by_real = dot_nt(both, matrix[0], precision)
    by_imag = dot_nt(both, matrix[1], precision)
    return jnp.stack([by_real[:n] + by_imag[n:], by_real[n:] - by_imag[:n]])


def combine_rows(coeffs, matrix, precision=HIGHEST):
    n = coeffs.shape[1]
    both = jnp.concatenate([coeffs[0], coeffs[1]], 0)
    by_real = jnp.dot(both, matrix[0], precision=precision, preferred_element_type=jnp.float32)
    by_imag = jnp.dot(both, matrix[1], precision=precision, preferred_element_type=jnp.float32)
    return jnp.stack([by_real[:n] - by_imag[n:], by_real[n:] + by_imag[:n]])


def index_of(z, y, x, c):
    return ((z * SIDE + y) * SIDE + x) * 2 + c


def move(value, target):
    pairs = []
    for z in range(SIDE):
        for y in range(SIDE):
            for x in range(SIDE):
                for c in range(2):
                    there = target(z, y, x, c)
                    if there is not None:
                        pairs.append((index_of(z, y, x, c), index_of(*there)))
    return lax.ppermute(value, AXES, pairs)


def swap(value):
    return lax.ppermute(value, "c", [(0, 1), (1, 0)])


def turn_y(value, offset):
    return move(value, lambda z, y, x, c: (z, (y - offset) % SIDE, x, c))


def hop(value, routes, idle=()):
    paired = dict(routes)
    spare = dict(zip(routes.values(), idle))
    for start, there in routes.items():
        if there in spare:
            paired[there] = spare[there]
            paired[spare[there]] = start
        else:
            paired[there] = start

    def target(z, y, x, c):
        there = paired.get((z, x))
        return (z, y, x, 1 - c) if there is None else (there[0], y, there[1], c)

    return move(value, target)


def local(factor, lower_inverse, upper_inverse, krylov_block, basis):
    z = lax.axis_index("z")
    y = lax.axis_index("y")
    x = lax.axis_index("x")
    c = lax.axis_index("c")
    piece = factor.shape[1]
    half = factor.shape[2]
    tile = 2 * half
    nvec = krylov_block.shape[1]
    nb = basis.shape[1]
    every = range(SIDE)

    def here(*places):
        found = jnp.zeros((), bool)
        for a, b in places:
            found = found | ((z == a) & (x == b))
        return found

    def rotated(value):
        return lax.dynamic_slice_in_dim(jnp.concatenate([value, value], 2), y * piece, tile, 2)

    def in_order(value, other):
        return jnp.concatenate([jnp.where(c == 0, value, other), jnp.where(c == 0, other, value)], 2)

    lower_half = lax.dynamic_slice_in_dim(lower_inverse, c * half, half, 1)
    upper_half = lax.dynamic_slice_in_dim(upper_inverse, c * half, half, 1)

    inverse = jnp.where(jnp.where(z == 0, x != 1, x == z - 1), lower_half, upper_half)
    left, right = factor[:, :, :piece], factor[:, :, piece:]
    packed = jnp.concatenate([left, right, inverse, krylov_block, basis], 1)
    pieces = [packed] + [turn_y(packed, d) for d in (1, 3, 2)]
    pieces = [pieces[0], pieces[1], pieces[3], pieces[2]]
    tall = jnp.concatenate([jnp.concatenate([p[:, :piece], p[:, piece:half]], 2) for p in pieces], 1)
    top = half + half
    rows = jnp.concatenate([p[:, half:top] for p in pieces], 2)
    given = jnp.concatenate([p[:, top:top + nvec] for p in pieces], 2)
    basis_all = jnp.stack([p[:, top + nvec:] for p in pieces])
    low = lax.dynamic_index_in_dim(basis_all, (2 * c - y) % SIDE, 0, False)
    high = lax.dynamic_index_in_dim(basis_all, (2 * c + 1 - y) % SIDE, 0, False)
    basis_half = jnp.concatenate([low, high], 2)

    plane = jnp.concatenate([basis_all[d] for d in every], 2)
    gram = herm_rows(plane, plane)

    empty = jnp.zeros((2, nvec, half), jnp.float32)
    small = jnp.zeros((2, nvec, nb), jnp.float32)
    blank = jnp.zeros((2, nvec, tile), jnp.float32)

    def product(places, vectors):
        return lax.cond(here(*places), apply_rows, lambda v, w: blank, vectors, tall)

    def finish(place, right, acc):
        other = swap(acc)

        def run(right, acc, other, weights):
            return apply_rows(right - (acc + other), weights)

        return lax.cond(here(place), run, lambda r, a, o, w: empty, right, acc, other, rows)

    def after(value, other):
        return lax.optimization_barrier((value, other))[0]

    def share(value, place):
        return lax.cond(here(place), herm_rows, lambda v, w: small, value, basis_half)

    starts = ((0, 0), (0, 2), (0, 3))
    y0 = lax.cond(here(*starts), apply_rows, lambda v, w: empty, given, rows)
    arrived = hop(y0, {(0, 0): (1, 0), (0, 2): (2, 0), (0, 3): (3, 0)})
    arrived, gram = lax.optimization_barrier((arrived, gram))
    acc0 = product(((1, 0),), arrived)
    y1 = finish((1, 0), given, acc0)
    near1 = hop(y1, {(1, 0): (2, 1)})
    far1 = hop(y1, {(1, 0): (3, 1)})
    near1, far1 = lax.optimization_barrier((near1, far1))
    early1 = hop(product(((2, 0), (3, 0)), after(arrived, y1)), {(2, 0): (2, 1), (3, 0): (3, 2)}, ((2, 2), (1, 1)))
    y2 = finish((2, 1), given, early1 + product(((2, 1),), near1))
    near2 = hop(y2, {(2, 1): (3, 2)})
    held1 = early1 + hop(product(((3, 1),), after(far1, y2)), {(3, 1): (3, 2)}, ((2, 2),))
    y3 = finish((3, 2), given, held1 + product(((3, 2),), near2))

    grams = [hop(after(gram, y1), {place: (0, 1)}) for place in ((1, 1), (2, 2), (3, 3))]
    y3, grams = lax.optimization_barrier((y3, grams))
    gram = gram + (grams[0] + grams[1] + grams[2])
    back = hop(y0 + y1 + y2 + y3, {(0, 0): (0, 1), (1, 0): (1, 2), (2, 1): (2, 3), (3, 2): (3, 3)})
    solved = rotated(in_order(back, swap(back)))

    x3 = lax.cond(here((3, 3)), apply_rows, lambda v, w: empty, solved, rows)
    near3 = hop(x3, {(3, 3): (2, 3)})
    far3 = hop(x3, {(3, 3): (1, 3)})
    x2 = finish((2, 3), solved, product(((2, 3),), near3))
    near4 = hop(x2 + x3, {(2, 3): (1, 2), (3, 3): (0, 3)})
    sent3 = hop(share(after(x3, x2), (3, 3)), {(3, 3): (0, 1)})
    sent2 = hop(share(x2, (2, 3)), {(2, 3): (0, 1)})
    far4 = hop(x2, {(2, 3): (0, 2)})
    near4, far4, sent2, sent3 = lax.optimization_barrier((near4, far4, sent2, sent3))
    side1 = hop(product(((1, 3),), after(far3, x2)), {(1, 3): (1, 2)}, ((1, 1),))
    x1 = finish((1, 2), solved, side1 + product(((1, 2),), near4))
    part1 = lax.cond(here((1, 2)), herm_rows, lambda v, w: small, x1, basis_half)
    near5 = hop(jnp.concatenate([x1, part1], 2), {(1, 2): (0, 1)})
    moved = hop(after(x1 + x2 + x3, part1), {(1, 2): (1, 1), (2, 3): (2, 1), (3, 3): (3, 1)})
    carried = near5[:, :, half:]
    side0 = hop(after(product(((0, 3),), near4), part1), {(0, 3): (0, 1)}, ((0, 0),))
    held3 = side0 + hop(after(product(((0, 2),), far4), part1), {(0, 2): (0, 1)}, ((2, 2),))
    sent = carried + sent2 + sent3
    near5 = near5[:, :, :half]
    x0 = finish((0, 1), solved, held3 + product(((0, 1),), near5))

    found = jnp.where(z == 0, x0, moved)
    sums = share(x0, (0, 1)) + sent
    both = jnp.concatenate([found, sums], 2)
    other = swap(both)
    first = sums + other[:, :, half:]
    coeffs = 2.0 * first - combine_rows(first, gram)
    far = [hop(coeffs, {(0, 1): (a, 1)}) for a in (2, 1, 3)]
    total = coeffs
    for a, landed in zip((2, 1, 3), far):
        total = jnp.where(z == a, landed, total)
    chosen = jnp.where((y < 2) == (c == 0), found, other[:, :, :half])
    mine = jnp.where(y % 2 == 0, chosen[:, :, :piece], chosen[:, :, piece:])
    message = jnp.concatenate([mine, total], 2)
    chain = message
    for d in (2, 1, 3):
        landed = hop(message, {(a, 1): (a, (1 + d) % SIDE) for a in every})
        chain = jnp.where(x == (1 + d) % SIDE, landed, chain)
    own_rows = chain[:, :, :piece]
    total = chain[:, :, piece:]
    projected = own_rows - combine_rows(total, basis)
    return projected, jnp.swapaxes(total, 1, 2)


def solution(mesh):
    split = Mesh(mesh.devices.reshape(SIDE, SIDE, SIDE, 2), AXES)
    row, col = ("z", "y"), ("x", "c")
    in_specs = (P(None, row, col), P(None, None, row), P(None, None, row), P(None, None, row), P(None, None, row))
    out_specs = (P(None, None, row), P())
    return jax.shard_map(local, mesh=split, in_specs=in_specs, out_specs=out_specs, check_vma=False)
```

```python
import jax
import jax.numpy as jnp
from jax import lax
from jax.sharding import Mesh, PartitionSpec as P

SIDE = 4
AXES = ("z", "y", "x", "c")
HIGH = lax.Precision.HIGH
HIGHEST = lax.Precision.HIGHEST


def dot_nt(left, right, precision):
    return lax.dot_general(left, right, (((1,), (1,)), ((), ())), precision=precision, preferred_element_type=jnp.float32)


def apply_rows(vectors, matrix, precision=HIGH):
    n = vectors.shape[1]
    both = jnp.concatenate([vectors[0], vectors[1]], 0)
    by_real = dot_nt(both, matrix[0], precision)
    by_imag = dot_nt(both, matrix[1], precision)
    return jnp.stack([by_real[:n] - by_imag[n:], by_real[n:] + by_imag[:n]])


def herm_rows(vectors, matrix, precision=HIGHEST):
    n = vectors.shape[1]
    both = jnp.concatenate([vectors[0], vectors[1]], 0)
    by_real = dot_nt(both, matrix[0], precision)
    by_imag = dot_nt(both, matrix[1], precision)
    return jnp.stack([by_real[:n] + by_imag[n:], by_real[n:] - by_imag[:n]])


def combine_rows(coeffs, matrix, precision=HIGHEST):
    n = coeffs.shape[1]
    both = jnp.concatenate([coeffs[0], coeffs[1]], 0)
    by_real = jnp.dot(both, matrix[0], precision=precision, preferred_element_type=jnp.float32)
    by_imag = jnp.dot(both, matrix[1], precision=precision, preferred_element_type=jnp.float32)
    return jnp.stack([by_real[:n] - by_imag[n:], by_real[n:] + by_imag[:n]])


def index_of(z, y, x, c):
    return ((z * SIDE + y) * SIDE + x) * 2 + c


def move(value, target):
    pairs = []
    for z in range(SIDE):
        for y in range(SIDE):
            for x in range(SIDE):
                for c in range(2):
                    there = target(z, y, x, c)
                    if there is not None:
                        pairs.append((index_of(z, y, x, c), index_of(*there)))
    return lax.ppermute(value, AXES, pairs)


def swap(value):
    return lax.ppermute(value, "c", [(0, 1), (1, 0)])


def turn_y(value, offset):
    return move(value, lambda z, y, x, c: (z, (y - offset) % SIDE, x, c))


def hop(value, routes, idle=()):
    paired = dict(routes)
    spare = dict(zip(routes.values(), idle))
    for start, there in routes.items():
        if there in spare:
            paired[there] = spare[there]
            paired[spare[there]] = start
        else:
            paired[there] = start

    def target(z, y, x, c):
        there = paired.get((z, x))
        return (z, y, x, 1 - c) if there is None else (there[0], y, there[1], c)

    return move(value, target)


def local(factor, lower_inverse, upper_inverse, krylov_block, basis):
    z = lax.axis_index("z")
    y = lax.axis_index("y")
    x = lax.axis_index("x")
    c = lax.axis_index("c")
    piece = factor.shape[1]
    half = factor.shape[2]
    tile = 2 * half
    nvec = krylov_block.shape[1]
    nb = basis.shape[1]
    every = range(SIDE)

    def here(*places):
        found = jnp.zeros((), bool)
        for a, b in places:
            found = found | ((z == a) & (x == b))
        return found

    def rotated(value):
        return lax.dynamic_slice_in_dim(jnp.concatenate([value, value], 2), y * piece, tile, 2)

    def in_order(value, other):
        return jnp.concatenate([jnp.where(c == 0, value, other), jnp.where(c == 0, other, value)], 2)

    lower_half = lax.dynamic_slice_in_dim(lower_inverse, c * half, half, 1)
    upper_half = lax.dynamic_slice_in_dim(upper_inverse, c * half, half, 1)

    inverse = jnp.where(jnp.where(z == 0, x != 1, x == z - 1), lower_half, upper_half)
    left, right = factor[:, :, :piece], factor[:, :, piece:]
    packed = jnp.concatenate([left, right, inverse, krylov_block, basis], 1)
    pieces = [packed] + [turn_y(packed, d) for d in (1, 3, 2)]
    pieces = [pieces[0], pieces[1], pieces[3], pieces[2]]
    tall = jnp.concatenate([jnp.concatenate([p[:, :piece], p[:, piece:half]], 2) for p in pieces], 1)
    top = half + half
    rows = jnp.concatenate([p[:, half:top] for p in pieces], 2)
    given = jnp.concatenate([p[:, top:top + nvec] for p in pieces], 2)
    basis_all = jnp.stack([p[:, top + nvec:] for p in pieces])
    low = lax.dynamic_index_in_dim(basis_all, (2 * c - y) % SIDE, 0, False)
    high = lax.dynamic_index_in_dim(basis_all, (2 * c + 1 - y) % SIDE, 0, False)
    basis_half = jnp.concatenate([low, high], 2)

    plane = jnp.concatenate([basis_all[d] for d in every], 2)
    gram = herm_rows(plane, plane)

    empty = jnp.zeros((2, nvec, half), jnp.float32)
    small = jnp.zeros((2, nvec, nb), jnp.float32)
    blank = jnp.zeros((2, nvec, tile), jnp.float32)

    def product(places, vectors):
        return lax.cond(here(*places), apply_rows, lambda v, w: blank, vectors, tall)

    def finish(place, right, acc):
        other = swap(acc)

        def run(right, acc, other, weights):
            return apply_rows(right - (acc + other), weights)

        return lax.cond(here(place), run, lambda r, a, o, w: empty, right, acc, other, rows)

    def after(value, other):
        return lax.optimization_barrier((value, other))[0]

    def share(value, place):
        return lax.cond(here(place), herm_rows, lambda v, w: small, value, basis_half)

    starts = ((0, 0), (0, 2), (0, 3))
    y0 = lax.cond(here(*starts), apply_rows, lambda v, w: empty, given, rows)
    arrived = hop(y0, {(0, 0): (1, 0), (0, 2): (2, 0), (0, 3): (3, 0)})
    arrived, gram = lax.optimization_barrier((arrived, gram))
    acc0 = product(((1, 0),), arrived)
    y1 = finish((1, 0), given, acc0)
    near1 = hop(y1, {(1, 0): (2, 1)})
    far1 = hop(y1, {(1, 0): (3, 1)})
    near1, far1 = lax.optimization_barrier((near1, far1))
    early1 = hop(product(((2, 0), (3, 0)), after(arrived, y1)), {(2, 0): (2, 1), (3, 0): (3, 2)}, ((2, 2), (1, 1)))
    y2 = finish((2, 1), given, early1 + product(((2, 1),), near1))
    near2 = hop(y2, {(2, 1): (3, 2)})
    held1 = early1 + hop(product(((3, 1),), after(far1, y2)), {(3, 1): (3, 2)}, ((0, 0),))
    y3 = finish((3, 2), given, held1 + product(((3, 2),), near2))

    sent1 = hop(after(gram, y1), {(1, 1): (0, 1)})
    back = hop(y0 + y1 + y2 + y3, {(0, 0): (0, 1), (1, 0): (1, 2), (2, 1): (2, 3), (3, 2): (3, 3)})
    solved = rotated(in_order(back, swap(back)))

    x3 = lax.cond(here((3, 3)), apply_rows, lambda v, w: empty, solved, rows)
    near3 = hop(x3, {(3, 3): (2, 3)})
    far3 = hop(x3, {(3, 3): (1, 3)})
    x2 = finish((2, 3), solved, product(((2, 3),), near3))
    near4 = hop(x2 + x3, {(2, 3): (1, 2), (3, 3): (0, 3)})
    far4 = hop(x2, {(2, 3): (0, 2)})
    share3 = jnp.concatenate([share(after(x3, x2), (3, 3)), gram], 1)
    share2 = jnp.concatenate([share(x2, (2, 3)), gram], 1)
    near4, far4, sent1, share3, share2 = lax.optimization_barrier((near4, far4, sent1, share3, share2))
    side1 = hop(product(((1, 3),), after(far3, x2)), {(1, 3): (1, 2)}, ((1, 1),))
    x1 = finish((1, 2), solved, side1 + product(((1, 2),), near4))
    part1 = lax.cond(here((1, 2)), herm_rows, lambda v, w: small, x1, basis_half)
    near5 = hop(jnp.concatenate([x1, part1], 2), {(1, 2): (0, 1)})
    sent3 = hop(after(share3, x1), {(3, 3): (0, 1)})
    sent2 = hop(after(share2, x1), {(2, 3): (0, 1)})
    near5, sent2, sent3 = lax.optimization_barrier((near5, sent2, sent3))
    moved = hop(after(x1 + x2 + x3, part1), {(1, 2): (1, 1), (2, 3): (2, 1), (3, 3): (3, 1)})
    carried = near5[:, :, half:]
    side0 = hop(after(product(((0, 3),), near4), part1), {(0, 3): (0, 1)}, ((0, 0),))
    held3 = side0 + hop(after(product(((0, 2),), far4), part1), {(0, 2): (0, 1)}, ((2, 2),))
    sent = carried + sent2[:, :nvec] + sent3[:, :nvec]
    gram = gram + sent1 + sent2[:, nvec:] + sent3[:, nvec:]
    near5 = near5[:, :, :half]
    x0 = finish((0, 1), solved, held3 + product(((0, 1),), near5))

    found = jnp.where(z == 0, x0, moved)
    sums = share(x0, (0, 1)) + sent
    both = jnp.concatenate([found, sums], 2)
    other = swap(both)
    first = sums + other[:, :, half:]
    coeffs = 2.0 * first - combine_rows(first, gram)
    far = [hop(coeffs, {(0, 1): (a, 1)}) for a in (2, 1, 3)]
    total = coeffs
    for a, landed in zip((2, 1, 3), far):
        total = jnp.where(z == a, landed, total)
    chosen = jnp.where((y < 2) == (c == 0), found, other[:, :, :half])
    mine = jnp.where(y % 2 == 0, chosen[:, :, :piece], chosen[:, :, piece:])
    message = jnp.concatenate([mine, total], 2)
    chain = message
    for d in (2, 1, 3):
        landed = hop(message, {(a, 1): (a, (1 + d) % SIDE) for a in every})
        chain = jnp.where(x == (1 + d) % SIDE, landed, chain)
    own_rows = chain[:, :, :piece]
    total = chain[:, :, piece:]
    projected = own_rows - combine_rows(total, basis)
    return projected, jnp.swapaxes(total, 1, 2)


def solution(mesh):
    split = Mesh(mesh.devices.reshape(SIDE, SIDE, SIDE, 2), AXES)
    row, col = ("z", "y"), ("x", "c")
    in_specs = (P(None, row, col), P(None, None, row), P(None, None, row), P(None, None, row), P(None, None, row))
    out_specs = (P(None, None, row), P())
    return jax.shard_map(local, mesh=split, in_specs=in_specs, out_specs=out_specs, check_vma=False)
```

```python
import jax
import jax.numpy as jnp
from jax import lax
from jax.sharding import Mesh, PartitionSpec as P

SIDE = 4
AXES = ("z", "y", "x", "c")
HIGH = lax.Precision.HIGH
HIGHEST = lax.Precision.HIGHEST


def dot_nt(left, right, precision):
    return lax.dot_general(left, right, (((1,), (1,)), ((), ())), precision=precision, preferred_element_type=jnp.float32)


def apply_rows(vectors, matrix, precision=HIGH):
    n = vectors.shape[1]
    both = jnp.concatenate([vectors[0], vectors[1]], 0)
    by_real = dot_nt(both, matrix[0], precision)
    by_imag = dot_nt(both, matrix[1], precision)
    return jnp.stack([by_real[:n] - by_imag[n:], by_real[n:] + by_imag[:n]])


def herm_rows(vectors, matrix, precision=HIGHEST):
    n = vectors.shape[1]
    both = jnp.concatenate([vectors[0], vectors[1]], 0)
    by_real = dot_nt(both, matrix[0], precision)
    by_imag = dot_nt(both, matrix[1], precision)
    return jnp.stack([by_real[:n] + by_imag[n:], by_real[n:] - by_imag[:n]])


def combine_rows(coeffs, matrix, precision=HIGHEST):
    n = coeffs.shape[1]
    both = jnp.concatenate([coeffs[0], coeffs[1]], 0)
    by_real = jnp.dot(both, matrix[0], precision=precision, preferred_element_type=jnp.float32)
    by_imag = jnp.dot(both, matrix[1], precision=precision, preferred_element_type=jnp.float32)
    return jnp.stack([by_real[:n] - by_imag[n:], by_real[n:] + by_imag[:n]])


def index_of(z, y, x, c):
    return ((z * SIDE + y) * SIDE + x) * 2 + c


def move(value, target):
    pairs = []
    for z in range(SIDE):
        for y in range(SIDE):
            for x in range(SIDE):
                for c in range(2):
                    there = target(z, y, x, c)
                    if there is not None:
                        pairs.append((index_of(z, y, x, c), index_of(*there)))
    return lax.ppermute(value, AXES, pairs)


def swap(value):
    return lax.ppermute(value, "c", [(0, 1), (1, 0)])


def turn_y(value, offset):
    return move(value, lambda z, y, x, c: (z, (y - offset) % SIDE, x, c))


def hop(value, routes, idle=()):
    paired = dict(routes)
    spare = dict(zip(routes.values(), idle))
    for start, there in routes.items():
        if there in spare:
            paired[there] = spare[there]
            paired[spare[there]] = start
        else:
            paired[there] = start

    def target(z, y, x, c):
        there = paired.get((z, x))
        return (z, y, x, 1 - c) if there is None else (there[0], y, there[1], c)

    return move(value, target)


def local(factor, lower_inverse, upper_inverse, krylov_block, basis):
    z = lax.axis_index("z")
    y = lax.axis_index("y")
    x = lax.axis_index("x")
    c = lax.axis_index("c")
    piece = factor.shape[1]
    half = factor.shape[2]
    tile = 2 * half
    nvec = krylov_block.shape[1]
    nb = basis.shape[1]
    every = range(SIDE)

    def here(*places):
        found = jnp.zeros((), bool)
        for a, b in places:
            found = found | ((z == a) & (x == b))
        return found

    def rotated(value):
        return lax.dynamic_slice_in_dim(jnp.concatenate([value, value], 2), y * piece, tile, 2)

    def in_order(value, other):
        return jnp.concatenate([jnp.where(c == 0, value, other), jnp.where(c == 0, other, value)], 2)

    lower_half = lax.dynamic_slice_in_dim(lower_inverse, c * half, half, 1)
    upper_half = lax.dynamic_slice_in_dim(upper_inverse, c * half, half, 1)

    inverse = jnp.where(jnp.where(z == 0, x != 1, x == z - 1), lower_half, upper_half)
    left, right = factor[:, :, :piece], factor[:, :, piece:]
    packed = jnp.concatenate([left, right, inverse, krylov_block, basis], 1)
    pieces = [packed] + [turn_y(packed, d) for d in (1, 3, 2)]
    pieces = [pieces[0], pieces[1], pieces[3], pieces[2]]
    tall = jnp.concatenate([jnp.concatenate([p[:, :piece], p[:, piece:half]], 2) for p in pieces], 1)
    top = half + half
    rows = jnp.concatenate([p[:, half:top] for p in pieces], 2)
    given = jnp.concatenate([p[:, top:top + nvec] for p in pieces], 2)
    basis_all = jnp.stack([p[:, top + nvec:] for p in pieces])
    low = lax.dynamic_index_in_dim(basis_all, (2 * c - y) % SIDE, 0, False)
    high = lax.dynamic_index_in_dim(basis_all, (2 * c + 1 - y) % SIDE, 0, False)
    basis_half = jnp.concatenate([low, high], 2)

    plane = jnp.concatenate([basis_all[d] for d in every], 2)
    gram = herm_rows(plane, plane)

    empty = jnp.zeros((2, nvec, half), jnp.float32)
    small = jnp.zeros((2, nvec, nb), jnp.float32)
    blank = jnp.zeros((2, nvec, tile), jnp.float32)

    def product(places, vectors):
        return lax.cond(here(*places), apply_rows, lambda v, w: blank, vectors, tall)

    def finish(place, right, acc):
        other = swap(acc)

        def run(right, acc, other, weights):
            return apply_rows(right - (acc + other), weights)

        return lax.cond(here(place), run, lambda r, a, o, w: empty, right, acc, other, rows)

    def after(value, other):
        return lax.optimization_barrier((value, other))[0]

    def share(value, place):
        return lax.cond(here(place), herm_rows, lambda v, w: small, value, basis_half)

    starts = ((0, 0), (0, 2), (0, 3))
    y0 = lax.cond(here(*starts), apply_rows, lambda v, w: empty, given, rows)
    arrived = hop(y0, {(0, 0): (1, 0), (0, 2): (2, 0), (0, 3): (3, 0)})
    arrived, gram = lax.optimization_barrier((arrived, gram))
    acc0 = product(((1, 0),), arrived)
    y1 = finish((1, 0), given, acc0)
    near1 = hop(y1, {(1, 0): (2, 1)})
    far1 = hop(y1, {(1, 0): (3, 1)})
    near1, far1 = lax.optimization_barrier((near1, far1))
    early1 = hop(product(((2, 0), (3, 0)), after(arrived, y1)), {(2, 0): (2, 1), (3, 0): (3, 2)}, ((2, 2), (1, 1)))
    y2 = finish((2, 1), given, early1 + product(((2, 1),), near1))
    near2 = hop(y2, {(2, 1): (3, 2)})
    held1 = early1 + hop(product(((3, 1),), after(far1, y2)), {(3, 1): (3, 2)}, ((0, 0),))
    y3 = finish((3, 2), given, held1 + product(((3, 2),), near2))

    grams = [hop(after(gram, y1), {place: (0, 1)}) for place in ((1, 1), (2, 2), (3, 3))]
    y3, grams = lax.optimization_barrier((y3, grams))
    gram = gram + (grams[0] + grams[1] + grams[2])
    back = hop(y0 + y1 + y2 + y3, {(0, 0): (0, 1), (1, 0): (1, 2), (2, 1): (2, 3), (3, 2): (3, 3)})
    solved = rotated(in_order(back, swap(back)))

    x3 = lax.cond(here((3, 3)), apply_rows, lambda v, w: empty, solved, rows)
    near3 = hop(x3, {(3, 3): (2, 3)})
    far3 = hop(x3, {(3, 3): (1, 3)})
    x2 = finish((2, 3), solved, product(((2, 3),), near3))
    near4 = hop(x2 + x3, {(2, 3): (1, 2), (3, 3): (0, 3)})
    side1 = hop(product(((1, 3),), after(far3, x2)), {(1, 3): (1, 2)}, ((1, 1),))
    far4 = hop(x2, {(2, 3): (0, 2)})
    x1 = finish((1, 2), solved, side1 + product(((1, 2),), near4))
    part1 = lax.cond(here((1, 2)), herm_rows, lambda v, w: small, x1, basis_half)
    near5 = hop(jnp.concatenate([x1, part1], 2), {(1, 2): (0, 1)})
    sent3 = hop(share(after(x3, part1), (3, 3)), {(3, 3): (0, 1)})
    sent2 = hop(share(after(x2, part1), (2, 3)), {(2, 3): (0, 1)})
    moved = hop(after(x1 + x2 + x3, part1), {(1, 2): (1, 1), (2, 3): (2, 1), (3, 3): (3, 1)})
    carried = near5[:, :, half:]
    side0 = hop(after(product(((0, 3),), near4), part1), {(0, 3): (0, 1)}, ((0, 0),))
    held3 = side0 + hop(after(product(((0, 2),), far4), part1), {(0, 2): (0, 1)}, ((2, 2),))
    sent = carried + sent2 + sent3
    near5 = near5[:, :, :half]
    x0 = finish((0, 1), solved, held3 + product(((0, 1),), near5))

    found = jnp.where(z == 0, x0, moved)
    sums = share(x0, (0, 1)) + sent
    both = jnp.concatenate([found, sums], 2)
    other = swap(both)
    first = sums + other[:, :, half:]
    coeffs = 2.0 * first - combine_rows(first, gram)
    far = [hop(coeffs, {(0, 1): (a, 1)}) for a in (2, 1, 3)]
    total = coeffs
    for a, landed in zip((2, 1, 3), far):
        total = jnp.where(z == a, landed, total)
    chosen = jnp.where((y < 2) == (c == 0), found, other[:, :, :half])
    mine = jnp.where(y % 2 == 0, chosen[:, :, :piece], chosen[:, :, piece:])
    message = jnp.concatenate([mine, total], 2)
    chain = message
    for d in (2, 1, 3):
        landed = hop(message, {(a, 1): (a, (1 + d) % SIDE) for a in every})
        chain = jnp.where(x == (1 + d) % SIDE, landed, chain)
    own_rows = chain[:, :, :piece]
    total = chain[:, :, piece:]
    projected = own_rows - combine_rows(total, basis)
    return projected, jnp.swapaxes(total, 1, 2)


def solution(mesh):
    split = Mesh(mesh.devices.reshape(SIDE, SIDE, SIDE, 2), AXES)
    row, col = ("z", "y"), ("x", "c")
    in_specs = (P(None, row, col), P(None, None, row), P(None, None, row), P(None, None, row), P(None, None, row))
    out_specs = (P(None, None, row), P())
    return jax.shard_map(local, mesh=split, in_specs=in_specs, out_specs=out_specs, check_vma=False)
```

```python
import jax
import jax.numpy as jnp
from jax import lax
from jax.sharding import Mesh, PartitionSpec as P

SIDE = 4
AXES = ("z", "y", "x", "c")
HIGH = lax.Precision.HIGH
HIGHEST = lax.Precision.HIGHEST


def dot_nt(left, right, precision):
    return lax.dot_general(left, right, (((1,), (1,)), ((), ())), precision=precision, preferred_element_type=jnp.float32)


def apply_rows(vectors, matrix, precision=HIGH):
    n = vectors.shape[1]
    both = jnp.concatenate([vectors[0], vectors[1]], 0)
    by_real = dot_nt(both, matrix[0], precision)
    by_imag = dot_nt(both, matrix[1], precision)
    return jnp.stack([by_real[:n] - by_imag[n:], by_real[n:] + by_imag[:n]])


def herm_rows(vectors, matrix, precision=HIGHEST):
    n = vectors.shape[1]
    both = jnp.concatenate([vectors[0], vectors[1]], 0)
    by_real = dot_nt(both, matrix[0], precision)
    by_imag = dot_nt(both, matrix[1], precision)
    return jnp.stack([by_real[:n] + by_imag[n:], by_real[n:] - by_imag[:n]])


def combine_rows(coeffs, matrix, precision=HIGHEST):
    n = coeffs.shape[1]
    both = jnp.concatenate([coeffs[0], coeffs[1]], 0)
    by_real = jnp.dot(both, matrix[0], precision=precision, preferred_element_type=jnp.float32)
    by_imag = jnp.dot(both, matrix[1], precision=precision, preferred_element_type=jnp.float32)
    return jnp.stack([by_real[:n] - by_imag[n:], by_real[n:] + by_imag[:n]])


def index_of(z, y, x, c):
    return ((z * SIDE + y) * SIDE + x) * 2 + c


def move(value, target):
    pairs = []
    for z in range(SIDE):
        for y in range(SIDE):
            for x in range(SIDE):
                for c in range(2):
                    there = target(z, y, x, c)
                    if there is not None:
                        pairs.append((index_of(z, y, x, c), index_of(*there)))
    return lax.ppermute(value, AXES, pairs)


def swap(value):
    return lax.ppermute(value, "c", [(0, 1), (1, 0)])


def turn_y(value, offset):
    return move(value, lambda z, y, x, c: (z, (y - offset) % SIDE, x, c))


def hop(value, routes, idle=()):
    paired = dict(routes)
    spare = dict(zip(routes.values(), idle))
    for start, there in routes.items():
        if there in spare:
            paired[there] = spare[there]
            paired[spare[there]] = start
        else:
            paired[there] = start

    def target(z, y, x, c):
        there = paired.get((z, x))
        return (z, y, x, 1 - c) if there is None else (there[0], y, there[1], c)

    return move(value, target)


def local(factor, lower_inverse, upper_inverse, krylov_block, basis):
    z = lax.axis_index("z")
    y = lax.axis_index("y")
    x = lax.axis_index("x")
    c = lax.axis_index("c")
    piece = factor.shape[1]
    half = factor.shape[2]
    tile = 2 * half
    nvec = krylov_block.shape[1]
    nb = basis.shape[1]
    every = range(SIDE)

    def here(*places):
        found = jnp.zeros((), bool)
        for a, b in places:
            found = found | ((z == a) & (x == b))
        return found

    def rotated(value):
        return lax.dynamic_slice_in_dim(jnp.concatenate([value, value], 2), y * piece, tile, 2)

    def in_order(value, other):
        return jnp.concatenate([jnp.where(c == 0, value, other), jnp.where(c == 0, other, value)], 2)

    lower_half = lax.dynamic_slice_in_dim(lower_inverse, c * half, half, 1)
    upper_half = lax.dynamic_slice_in_dim(upper_inverse, c * half, half, 1)

    inverse = jnp.where(jnp.where(z == 0, x != 1, x == z - 1), lower_half, upper_half)
    left, right = factor[:, :, :piece], factor[:, :, piece:]
    packed = jnp.concatenate([left, right, inverse, krylov_block, basis], 1)
    pieces = [packed] + [turn_y(packed, d) for d in (1, 3, 2)]
    pieces = [pieces[0], pieces[1], pieces[3], pieces[2]]
    tall = jnp.concatenate([jnp.concatenate([p[:, :piece], p[:, piece:half]], 2) for p in pieces], 1)
    top = half + half
    rows = jnp.concatenate([p[:, half:top] for p in pieces], 2)
    given = jnp.concatenate([p[:, top:top + nvec] for p in pieces], 2)
    basis_all = jnp.stack([p[:, top + nvec:] for p in pieces])
    low = lax.dynamic_index_in_dim(basis_all, (2 * c - y) % SIDE, 0, False)
    high = lax.dynamic_index_in_dim(basis_all, (2 * c + 1 - y) % SIDE, 0, False)
    basis_half = jnp.concatenate([low, high], 2)

    plane = jnp.concatenate([basis_all[d] for d in every], 2)
    gram = herm_rows(plane, plane)

    empty = jnp.zeros((2, nvec, half), jnp.float32)
    small = jnp.zeros((2, nvec, nb), jnp.float32)
    blank = jnp.zeros((2, nvec, tile), jnp.float32)

    def product(places, vectors):
        return lax.cond(here(*places), apply_rows, lambda v, w: blank, vectors, tall)

    def finish(place, right, acc):
        other = swap(acc)

        def run(right, acc, other, weights):
            return apply_rows(right - (acc + other), weights)

        return lax.cond(here(place), run, lambda r, a, o, w: empty, right, acc, other, rows)

    def after(value, other):
        return lax.optimization_barrier((value, other))[0]

    def share(value, place):
        return lax.cond(here(place), herm_rows, lambda v, w: small, value, basis_half)

    starts = ((0, 0), (0, 2), (0, 3))
    y0 = lax.cond(here(*starts), apply_rows, lambda v, w: empty, given, rows)
    arrived = hop(y0, {(0, 0): (1, 0), (0, 2): (2, 0), (0, 3): (3, 0)})
    arrived, gram = lax.optimization_barrier((arrived, gram))
    acc0 = product(((1, 0),), arrived)
    y1 = finish((1, 0), given, acc0)
    near1 = hop(y1, {(1, 0): (2, 1)})
    far1 = hop(y1, {(1, 0): (3, 1)})
    near1, far1 = lax.optimization_barrier((near1, far1))
    early1 = hop(product(((2, 0), (3, 0)), after(arrived, y1)), {(2, 0): (2, 1), (3, 0): (3, 2)}, ((2, 2), (1, 1)))
    y2 = finish((2, 1), given, early1 + product(((2, 1),), near1))
    near2 = hop(y2, {(2, 1): (3, 2)})
    held1 = early1 + hop(product(((3, 1),), after(far1, y2)), {(3, 1): (3, 2)}, ((0, 0),))
    y3 = finish((3, 2), given, held1 + product(((3, 2),), near2))

    grams = [hop(after(gram, y1), {place: (0, 1)}) for place in ((1, 1), (2, 2), (3, 3))]
    y3, grams = lax.optimization_barrier((y3, grams))
    gram = gram + (grams[0] + grams[1] + grams[2])
    back = hop(y0 + y1 + y2 + y3, {(0, 0): (0, 1), (1, 0): (1, 2), (2, 1): (2, 3), (3, 2): (3, 3)})
    solved = rotated(in_order(back, swap(back)))

    x3 = lax.cond(here((3, 3)), apply_rows, lambda v, w: empty, solved, rows)
    near3 = hop(x3, {(3, 3): (2, 3)})
    far3 = hop(x3, {(3, 3): (1, 3)})
    x2 = finish((2, 3), solved, product(((2, 3),), near3))
    near4 = hop(x2 + x3, {(2, 3): (1, 2), (3, 3): (0, 3)})
    side1 = hop(product(((1, 3),), after(far3, x2)), {(1, 3): (1, 2)}, ((1, 1),))
    far4 = hop(x2, {(2, 3): (0, 2)})
    x1 = finish((1, 2), solved, side1 + product(((1, 2),), near4))
    part1 = lax.cond(here((1, 2)), herm_rows, lambda v, w: small, x1, basis_half)
    near5 = hop(jnp.concatenate([x1, part1], 2), {(1, 2): (0, 1)}, ((0, 0),))
    sent3 = hop(after(share(after(x3, x2), (3, 3)), x1), {(3, 3): (0, 1)})
    sent2 = hop(after(share(x2, (2, 3)), x1), {(2, 3): (0, 1)})
    moved = hop(after(x1 + x2 + x3, part1), {(1, 2): (1, 1), (2, 3): (2, 1), (3, 3): (3, 1)})
    carried = near5[:, :, half:]
    side0 = hop(after(product(((0, 3),), near4), part1), {(0, 3): (0, 1)}, ((0, 0),))
    held3 = side0 + hop(after(product(((0, 2),), far4), part1), {(0, 2): (0, 1)}, ((2, 2),))
    sent = carried + sent2 + sent3
    near5 = after(near5[:, :, :half], (sent2, sent3))
    x0 = finish((0, 1), solved, held3 + product(((0, 1),), near5))

    found = jnp.where(z == 0, x0, moved)
    sums = share(x0, (0, 1)) + sent
    both = jnp.concatenate([found, sums], 2)
    other = swap(both)
    first = sums + other[:, :, half:]
    coeffs = 2.0 * first - combine_rows(first, gram)
    far = [hop(coeffs, {(0, 1): (a, 1)}) for a in (2, 1, 3)]
    total = coeffs
    for a, landed in zip((2, 1, 3), far):
        total = jnp.where(z == a, landed, total)
    chosen = jnp.where((y < 2) == (c == 0), found, other[:, :, :half])
    mine = jnp.where(y % 2 == 0, chosen[:, :, :piece], chosen[:, :, piece:])
    message = jnp.concatenate([mine, total], 2)
    chain = message
    for d in (2, 1, 3):
        landed = hop(message, {(a, 1): (a, (1 + d) % SIDE) for a in every})
        chain = jnp.where(x == (1 + d) % SIDE, landed, chain)
    own_rows = chain[:, :, :piece]
    total = chain[:, :, piece:]
    projected = own_rows - combine_rows(total, basis)
    return projected, jnp.swapaxes(total, 1, 2)


def solution(mesh):
    split = Mesh(mesh.devices.reshape(SIDE, SIDE, SIDE, 2), AXES)
    row, col = ("z", "y"), ("x", "c")
    in_specs = (P(None, row, col), P(None, None, row), P(None, None, row), P(None, None, row), P(None, None, row))
    out_specs = (P(None, None, row), P())
    return jax.shard_map(local, mesh=split, in_specs=in_specs, out_specs=out_specs, check_vma=False)
```

```python
import jax
import jax.numpy as jnp
from jax import lax
from jax.sharding import Mesh, PartitionSpec as P

SIDE = 4
AXES = ("z", "y", "x", "c")
HIGH = lax.Precision.HIGH
HIGHEST = lax.Precision.HIGHEST


def dot_nt(left, right, precision):
    return lax.dot_general(left, right, (((1,), (1,)), ((), ())), precision=precision, preferred_element_type=jnp.float32)


def apply_rows(vectors, matrix, precision=HIGH):
    n = vectors.shape[1]
    both = jnp.concatenate([vectors[0], vectors[1]], 0)
    by_real = dot_nt(both, matrix[0], precision)
    by_imag = dot_nt(both, matrix[1], precision)
    return jnp.stack([by_real[:n] - by_imag[n:], by_real[n:] + by_imag[:n]])


def herm_rows(vectors, matrix, precision=HIGHEST):
    n = vectors.shape[1]
    both = jnp.concatenate([vectors[0], vectors[1]], 0)
    by_real = dot_nt(both, matrix[0], precision)
    by_imag = dot_nt(both, matrix[1], precision)
    return jnp.stack([by_real[:n] + by_imag[n:], by_real[n:] - by_imag[:n]])


def combine_rows(coeffs, matrix, precision=HIGHEST):
    n = coeffs.shape[1]
    both = jnp.concatenate([coeffs[0], coeffs[1]], 0)
    by_real = jnp.dot(both, matrix[0], precision=precision, preferred_element_type=jnp.float32)
    by_imag = jnp.dot(both, matrix[1], precision=precision, preferred_element_type=jnp.float32)
    return jnp.stack([by_real[:n] - by_imag[n:], by_real[n:] + by_imag[:n]])


def index_of(z, y, x, c):
    return ((z * SIDE + y) * SIDE + x) * 2 + c


def move(value, target):
    pairs = []
    for z in range(SIDE):
        for y in range(SIDE):
            for x in range(SIDE):
                for c in range(2):
                    there = target(z, y, x, c)
                    if there is not None:
                        pairs.append((index_of(z, y, x, c), index_of(*there)))
    return lax.ppermute(value, AXES, pairs)


def swap(value):
    return lax.ppermute(value, "c", [(0, 1), (1, 0)])


def turn_y(value, offset):
    return move(value, lambda z, y, x, c: (z, (y - offset) % SIDE, x, c))


def hop(value, routes, idle=()):
    paired = dict(routes)
    spare = dict(zip(routes.values(), idle))
    for start, there in routes.items():
        if there in spare:
            paired[there] = spare[there]
            paired[spare[there]] = start
        else:
            paired[there] = start

    def target(z, y, x, c):
        there = paired.get((z, x))
        return (z, y, x, 1 - c) if there is None else (there[0], y, there[1], c)

    return move(value, target)


def local(factor, lower_inverse, upper_inverse, krylov_block, basis):
    z = lax.axis_index("z")
    y = lax.axis_index("y")
    x = lax.axis_index("x")
    c = lax.axis_index("c")
    piece = factor.shape[1]
    half = factor.shape[2]
    tile = 2 * half
    nvec = krylov_block.shape[1]
    nb = basis.shape[1]
    every = range(SIDE)

    def here(*places):
        found = jnp.zeros((), bool)
        for a, b in places:
            found = found | ((z == a) & (x == b))
        return found

    def rotated(value):
        return lax.dynamic_slice_in_dim(jnp.concatenate([value, value], 2), y * piece, tile, 2)

    def in_order(value, other):
        return jnp.concatenate([jnp.where(c == 0, value, other), jnp.where(c == 0, other, value)], 2)

    lower_half = lax.dynamic_slice_in_dim(lower_inverse, c * half, half, 1)
    upper_half = lax.dynamic_slice_in_dim(upper_inverse, c * half, half, 1)

    inverse = jnp.where(jnp.where(z == 0, x != 1, x == z - 1), lower_half, upper_half)
    left, right = factor[:, :, :piece], factor[:, :, piece:]
    packed = jnp.concatenate([left, right, inverse, krylov_block, basis], 1)
    pieces = [packed] + [turn_y(packed, d) for d in (1, 3, 2)]
    pieces = [pieces[0], pieces[1], pieces[3], pieces[2]]
    tall = jnp.concatenate([jnp.concatenate([p[:, :piece], p[:, piece:half]], 2) for p in pieces], 1)
    top = half + half
    rows = jnp.concatenate([p[:, half:top] for p in pieces], 2)
    given = jnp.concatenate([p[:, top:top + nvec] for p in pieces], 2)
    basis_all = jnp.stack([p[:, top + nvec:] for p in pieces])
    low = lax.dynamic_index_in_dim(basis_all, (2 * c - y) % SIDE, 0, False)
    high = lax.dynamic_index_in_dim(basis_all, (2 * c + 1 - y) % SIDE, 0, False)
    basis_half = jnp.concatenate([low, high], 2)

    plane = jnp.concatenate([basis_all[d] for d in every], 2)
    gram = herm_rows(plane, plane)

    empty = jnp.zeros((2, nvec, half), jnp.float32)
    small = jnp.zeros((2, nvec, nb), jnp.float32)
    blank = jnp.zeros((2, nvec, tile), jnp.float32)

    def product(places, vectors):
        return lax.cond(here(*places), apply_rows, lambda v, w: blank, vectors, tall)

    def finish(place, right, acc):
        other = swap(acc)

        def run(right, acc, other, weights):
            return apply_rows(right - (acc + other), weights)

        return lax.cond(here(place), run, lambda r, a, o, w: empty, right, acc, other, rows)

    def after(value, other):
        return lax.optimization_barrier((value, other))[0]

    def share(value, place):
        part = lax.cond(here(place), herm_rows, lambda v, w: small, value, basis_half)
        return jnp.concatenate([part, gram], 1)

    starts = ((0, 0), (0, 2), (0, 3))
    y0 = lax.cond(here(*starts), apply_rows, lambda v, w: empty, given, rows)
    arrived = hop(y0, {(0, 0): (1, 0), (0, 2): (2, 0), (0, 3): (3, 0)})
    arrived, gram = lax.optimization_barrier((arrived, gram))
    acc0 = product(((1, 0),), arrived)
    y1 = finish((1, 0), given, acc0)
    near1 = hop(y1, {(1, 0): (2, 1)})
    far1 = hop(y1, {(1, 0): (3, 1)})
    near1, far1 = lax.optimization_barrier((near1, far1))
    early1 = hop(product(((2, 0), (3, 0)), after(arrived, y1)), {(2, 0): (2, 1), (3, 0): (3, 2)}, ((2, 2), (1, 1)))
    y2 = finish((2, 1), given, early1 + product(((2, 1),), near1))
    near2 = hop(y2, {(2, 1): (3, 2)})
    held1 = early1 + hop(product(((3, 1),), after(far1, y2)), {(3, 1): (3, 2)}, ((2, 2),))
    y3 = finish((3, 2), given, held1 + product(((3, 2),), near2))

    sent1 = hop(after(gram, y1), {(1, 2): (0, 1)})
    y3, sent1 = lax.optimization_barrier((y3, sent1))
    back = hop(y0 + y1 + y2 + y3, {(0, 0): (0, 1), (1, 0): (1, 2), (2, 1): (2, 3), (3, 2): (3, 3)})
    solved = rotated(in_order(back, swap(back)))

    x3 = lax.cond(here((3, 3)), apply_rows, lambda v, w: empty, solved, rows)
    near3 = hop(x3, {(3, 3): (2, 3)})
    far3 = hop(x3, {(3, 3): (1, 3)})
    x2 = finish((2, 3), solved, product(((2, 3),), near3))
    near4 = hop(x2 + x3, {(2, 3): (1, 2), (3, 3): (0, 3)})
    side1 = hop(product(((1, 3),), after(far3, x2)), {(1, 3): (1, 2)}, ((1, 1),))
    far4 = hop(x2, {(2, 3): (0, 2)})
    share3, share2 = share(x3, (3, 3)), share(x2, (2, 3))
    x1 = finish((1, 2), solved, side1 + product(((1, 2),), near4))
    sent3 = hop(after(share3, x1), {(3, 3): (0, 1)})
    sent2 = hop(after(share2, x1), {(2, 3): (0, 1)})
    part1 = lax.cond(here((1, 2)), herm_rows, lambda v, w: small, x1, basis_half)
    near5 = hop(jnp.concatenate([x1, part1], 2), {(1, 2): (0, 1)})
    part1 = near5[:, :, half:]
    side0 = hop(after(product(((0, 3),), near4), x1), {(0, 3): (0, 1)}, ((0, 0),))
    held3 = side0 + hop(after(product(((0, 2),), far4), x1), {(0, 2): (0, 1)}, ((2, 2),))
    sent = jnp.concatenate([part1 + sent2[:, :nvec] + sent3[:, :nvec], sent1 + sent2[:, nvec:] + sent3[:, nvec:]], 1)
    near5 = near5[:, :, :half]
    x0 = finish((0, 1), solved, held3 + product(((0, 1),), near5))

    found = x0 + x1 + x2 + x3
    sums = share(x0, (0, 1)) + sent
    both = jnp.concatenate([found, sums[:, :nvec]], 2)
    other = swap(both)
    first = sums[:, :nvec] + other[:, :, half:]
    coeffs = 2.0 * first - combine_rows(first, sums[:, nvec:])
    chosen = jnp.where((y < 2) == (c == 0), found, other[:, :, :half])
    mine = jnp.where(y % 2 == 0, chosen[:, :, :piece], chosen[:, :, piece:])
    message = jnp.concatenate([mine, coeffs], 2)
    columns = (1, 2, 3, 3)
    column = jnp.where(z == 0, 1, jnp.where(z == 1, 2, 3))
    for d in (1, 3, 2):
        landed = hop(message, {(a, columns[a]): (a, (columns[a] + d) % SIDE) for a in every})
        if d == 1:
            chain = jnp.where(x == column, message, landed)
        else:
            chain = jnp.where(x == (column + d) % SIDE, landed, chain)
    own_rows = chain[:, :, :piece]
    coeffs = chain[:, :, piece:]
    total = coeffs
    for a in (1, 3, 2):
        landed = hop(coeffs, {(0, b): (a, b) for b in every})
        total = jnp.where(z == a, landed, total)
    projected = own_rows - combine_rows(total, basis)
    return projected, jnp.swapaxes(total, 1, 2)


def solution(mesh):
    split = Mesh(mesh.devices.reshape(SIDE, SIDE, SIDE, 2), AXES)
    row, col = ("z", "y"), ("x", "c")
    in_specs = (P(None, row, col), P(None, None, row), P(None, None, row), P(None, None, row), P(None, None, row))
    out_specs = (P(None, None, row), P())
    return jax.shard_map(local, mesh=split, in_specs=in_specs, out_specs=out_specs, check_vma=False)
```

```python
import jax
import jax.numpy as jnp
from jax import lax
from jax.sharding import Mesh, PartitionSpec as P

SIDE = 4
AXES = ("z", "y", "x", "c")
HIGH = lax.Precision.HIGH
HIGHEST = lax.Precision.HIGHEST


def dot_nt(left, right, precision):
    return lax.dot_general(left, right, (((1,), (1,)), ((), ())), precision=precision, preferred_element_type=jnp.float32)


def apply_rows(vectors, matrix, precision=HIGH):
    n = vectors.shape[1]
    both = jnp.concatenate([vectors[0], vectors[1]], 0)
    by_real = dot_nt(both, matrix[0], precision)
    by_imag = dot_nt(both, matrix[1], precision)
    return jnp.stack([by_real[:n] - by_imag[n:], by_real[n:] + by_imag[:n]])


def herm_rows(vectors, matrix, precision=HIGHEST):
    n = vectors.shape[1]
    both = jnp.concatenate([vectors[0], vectors[1]], 0)
    by_real = dot_nt(both, matrix[0], precision)
    by_imag = dot_nt(both, matrix[1], precision)
    return jnp.stack([by_real[:n] + by_imag[n:], by_real[n:] - by_imag[:n]])


def combine_rows(coeffs, matrix, precision=HIGHEST):
    n = coeffs.shape[1]
    both = jnp.concatenate([coeffs[0], coeffs[1]], 0)
    by_real = jnp.dot(both, matrix[0], precision=precision, preferred_element_type=jnp.float32)
    by_imag = jnp.dot(both, matrix[1], precision=precision, preferred_element_type=jnp.float32)
    return jnp.stack([by_real[:n] - by_imag[n:], by_real[n:] + by_imag[:n]])


def index_of(z, y, x, c):
    return ((z * SIDE + y) * SIDE + x) * 2 + c


def move(value, target):
    pairs = []
    for z in range(SIDE):
        for y in range(SIDE):
            for x in range(SIDE):
                for c in range(2):
                    there = target(z, y, x, c)
                    if there is not None:
                        pairs.append((index_of(z, y, x, c), index_of(*there)))
    return lax.ppermute(value, AXES, pairs)


def swap(value):
    return lax.ppermute(value, "c", [(0, 1), (1, 0)])


def turn_y(value, offset):
    return move(value, lambda z, y, x, c: (z, (y - offset) % SIDE, x, c))


def hop(value, routes, idle=()):
    paired = dict(routes)
    spare = dict(zip(routes.values(), idle))
    for start, there in routes.items():
        if there in spare:
            paired[there] = spare[there]
            paired[spare[there]] = start
        else:
            paired[there] = start

    def target(z, y, x, c):
        there = paired.get((z, x))
        return (z, y, x, 1 - c) if there is None else (there[0], y, there[1], c)

    return move(value, target)


def local(factor, lower_inverse, upper_inverse, krylov_block, basis):
    z = lax.axis_index("z")
    y = lax.axis_index("y")
    x = lax.axis_index("x")
    c = lax.axis_index("c")
    piece = factor.shape[1]
    half = factor.shape[2]
    tile = 2 * half
    nvec = krylov_block.shape[1]
    nb = basis.shape[1]
    every = range(SIDE)

    def here(*places):
        found = jnp.zeros((), bool)
        for a, b in places:
            found = found | ((z == a) & (x == b))
        return found

    def rotated(value):
        return lax.dynamic_slice_in_dim(jnp.concatenate([value, value], 2), y * piece, tile, 2)

    def in_order(value, other):
        return jnp.concatenate([jnp.where(c == 0, value, other), jnp.where(c == 0, other, value)], 2)

    lower_half = lax.dynamic_slice_in_dim(lower_inverse, c * half, half, 1)
    upper_half = lax.dynamic_slice_in_dim(upper_inverse, c * half, half, 1)

    inverse = jnp.where(jnp.where(z == 0, x != 1, x == z - 1), lower_half, upper_half)
    left, right = factor[:, :, :piece], factor[:, :, piece:]
    packed = jnp.concatenate([left, right, inverse, krylov_block, basis], 1)
    pieces = [packed] + [turn_y(packed, d) for d in (1, 3, 2)]
    pieces = [pieces[0], pieces[1], pieces[3], pieces[2]]
    tall = jnp.concatenate([jnp.concatenate([p[:, :piece], p[:, piece:half]], 2) for p in pieces], 1)
    top = half + half
    rows = jnp.concatenate([p[:, half:top] for p in pieces], 2)
    given = jnp.concatenate([p[:, top:top + nvec] for p in pieces], 2)
    basis_all = jnp.stack([p[:, top + nvec:] for p in pieces])
    low = lax.dynamic_index_in_dim(basis_all, (2 * c - y) % SIDE, 0, False)
    high = lax.dynamic_index_in_dim(basis_all, (2 * c + 1 - y) % SIDE, 0, False)
    basis_half = jnp.concatenate([low, high], 2)

    plane = jnp.concatenate([basis_all[d] for d in every], 2)
    gram = herm_rows(plane, plane)

    empty = jnp.zeros((2, nvec, half), jnp.float32)
    small = jnp.zeros((2, nvec, nb), jnp.float32)
    blank = jnp.zeros((2, nvec, tile), jnp.float32)

    def product(places, vectors):
        return lax.cond(here(*places), apply_rows, lambda v, w: blank, vectors, tall)

    def finish(place, right, acc):
        other = swap(acc)

        def run(right, acc, other, weights):
            return apply_rows(right - (acc + other), weights)

        return lax.cond(here(place), run, lambda r, a, o, w: empty, right, acc, other, rows)

    def after(value, other):
        return lax.optimization_barrier((value, other))[0]

    def share(value, place):
        part = lax.cond(here(place), herm_rows, lambda v, w: small, value, basis_half)
        return jnp.concatenate([part, gram], 1)

    starts = ((0, 0), (0, 2), (0, 3))
    y0 = lax.cond(here(*starts), apply_rows, lambda v, w: empty, given, rows)
    arrived = hop(y0, {(0, 0): (1, 0), (0, 2): (2, 0), (0, 3): (3, 0)})
    arrived, gram = lax.optimization_barrier((arrived, gram))
    acc0 = product(((1, 0),), arrived)
    y1 = finish((1, 0), given, acc0)
    near1 = hop(y1, {(1, 0): (2, 1)})
    far1 = hop(y1, {(1, 0): (3, 1)})
    near1, far1 = lax.optimization_barrier((near1, far1))
    early1 = hop(product(((2, 0), (3, 0)), after(arrived, y1)), {(2, 0): (2, 1), (3, 0): (3, 2)}, ((2, 2), (1, 1)))
    y2 = finish((2, 1), given, early1 + product(((2, 1),), near1))
    near2 = hop(y2, {(2, 1): (3, 2)})
    held1 = early1 + hop(product(((3, 1),), after(far1, y2)), {(3, 1): (3, 2)}, ((2, 2),))
    y3 = finish((3, 2), given, held1 + product(((3, 2),), near2))

    sent1 = hop(after(gram, y1), {(1, 2): (0, 1)})
    y3, sent1 = lax.optimization_barrier((y3, sent1))
    back = hop(y0 + y1 + y2 + y3, {(0, 0): (0, 1), (1, 0): (1, 2), (2, 1): (2, 3), (3, 2): (3, 3)})
    solved = rotated(in_order(back, swap(back)))

    x3 = lax.cond(here((3, 3)), apply_rows, lambda v, w: empty, solved, rows)
    near3 = hop(x3, {(3, 3): (2, 3)})
    far3 = hop(x3, {(3, 3): (1, 3)})
    x2 = finish((2, 3), solved, product(((2, 3),), near3))
    near4 = hop(x2 + x3, {(2, 3): (1, 2), (3, 3): (0, 3)})
    side1 = hop(product(((1, 3),), after(far3, x2)), {(1, 3): (1, 2)}, ((1, 1),))
    far4 = hop(x2, {(2, 3): (0, 2)})
    sent3 = hop(after(share(x3, (3, 3)), x2), {(3, 3): (0, 1)})
    sent2 = hop(share(x2, (2, 3)), {(2, 3): (0, 1)})
    x1 = finish((1, 2), after(solved, (sent2, sent3)), side1 + product(((1, 2),), near4))
    part1 = lax.cond(here((1, 2)), herm_rows, lambda v, w: small, x1, basis_half)
    near5 = hop(jnp.concatenate([x1, part1], 2), {(1, 2): (0, 1)})
    part1 = near5[:, :, half:]
    side0 = hop(after(product(((0, 3),), near4), x1), {(0, 3): (0, 1)}, ((0, 0),))
    held3 = side0 + hop(after(product(((0, 2),), far4), x1), {(0, 2): (0, 1)}, ((1, 1),))
    sent = jnp.concatenate([part1 + sent2[:, :nvec] + sent3[:, :nvec], sent1 + sent2[:, nvec:] + sent3[:, nvec:]], 1)
    near5 = near5[:, :, :half]
    x0 = finish((0, 1), solved, held3 + product(((0, 1),), near5))

    found = x0 + x1 + x2 + x3
    sums = share(x0, (0, 1)) + sent
    both = jnp.concatenate([found, sums[:, :nvec]], 2)
    other = swap(both)
    first = sums[:, :nvec] + other[:, :, half:]
    coeffs = 2.0 * first - combine_rows(first, sums[:, nvec:])
    chosen = jnp.where((y < 2) == (c == 0), found, other[:, :, :half])
    mine = jnp.where(y % 2 == 0, chosen[:, :, :piece], chosen[:, :, piece:])
    message = jnp.concatenate([mine, coeffs], 2)
    columns = (1, 2, 3, 3)
    column = jnp.where(z == 0, 1, jnp.where(z == 1, 2, 3))
    for d in (1, 3, 2):
        landed = hop(message, {(a, columns[a]): (a, (columns[a] + d) % SIDE) for a in every})
        if d == 1:
            chain = jnp.where(x == column, message, landed)
        else:
            chain = jnp.where(x == (column + d) % SIDE, landed, chain)
    own_rows = chain[:, :, :piece]
    coeffs = chain[:, :, piece:]
    total = coeffs
    for a in (1, 3, 2):
        landed = hop(coeffs, {(0, b): (a, b) for b in every})
        total = jnp.where(z == a, landed, total)
    projected = own_rows - combine_rows(total, basis)
    return projected, jnp.swapaxes(total, 1, 2)


def solution(mesh):
    split = Mesh(mesh.devices.reshape(SIDE, SIDE, SIDE, 2), AXES)
    row, col = ("z", "y"), ("x", "c")
    in_specs = (P(None, row, col), P(None, None, row), P(None, None, row), P(None, None, row), P(None, None, row))
    out_specs = (P(None, None, row), P())
    return jax.shard_map(local, mesh=split, in_specs=in_specs, out_specs=out_specs, check_vma=False)
```
